512 devices in a mesh: group: 4 (over x_hi, core), ans: 32 (over x_lo, z), tp: 4 (over y).
Axes of the slice: x: 4 (x_hi: 2, x_lo: 2; x = x_hi * 2 + x_lo), y: 4, z: 16, core: 2. Of those that a mesh axis runs over, the one named last changes fastest.
Arguments:
- q_ans: bfloat16 [16384, 4096], P(('group', 'ans'), 'tp'), parts along dimension 0, may hold values from -160 to 160
- kv_ans: bfloat16 [2, 16384, 512], P(None, ('group', 'ans'), 'tp'), parts along dimension 1, may hold values from -6 to 6
- q_prompt: bfloat16 [8192, 4096], P(('group', 'ans'), 'tp'), parts along dimension 0, may hold values from -160 to 160
- kv_prompt: bfloat16 [2, 8192, 512], P(None, ('group', 'ans'), 'tp'), parts along dimension 1, may hold values from -8 to 8
- dout_ans: bfloat16 [16384, 4096], P(('group', 'ans'), 'tp'), parts along dimension 0, may hold values from -48 to 48
- dout_prompt: bfloat16 [8192, 4096], P(('group', 'ans'), 'tp'), parts along dimension 0, may hold values from -48 to 48
- ans_len: int32 [128], P(('group', 'ans')), parts along dimension 0, may hold values from 32 to 128, as said below
- prompt_len: int32 [4], P('group'), parts along dimension 0, may hold values from 512 to 2048
Outputs:
- d_q_ans: bfloat16 [16384, 4096], P(('group', 'ans'), 'tp'), parts along dimension 0
- d_kv_ans: bfloat16 [2, 16384, 512], P(None, ('group', 'ans'), 'tp'), parts along dimension 1
- d_q_prompt: bfloat16 [8192, 4096], P(('group', 'ans'), 'tp'), parts along dimension 0
- d_kv_prompt: bfloat16 [2, 8192, 512], P(None, ('group', 'ans'), 'tp'), parts along dimension 1
The draws below stay inside these ranges and needn't reach their ends.
There are 4 independent parts, one for each index of `group`. The reference program is written for one: setup_inputs(seed, part) draws one part's arguments, and reference() takes and returns one part's arrays. A program takes and returns all parts, laid end to end along the dimension named above; each array names one. Nothing has to cross between parts.
Inputs may be any that keep to these rules, and one draw needn't show every extreme that they name: `ans_len`: in every draw some answer has length 128.
All inputs are finite; a program needn't handle non-finite values.
Results may differ from the reference program's by a relative error of at most 0.015.
Values may be sent and summed in bfloat16 or wider, within the bound.
A program may use at most 128 MiB of HBM per device.

```python
import math
import jax
import jax.numpy as jnp
from jax import lax

HQ = 32
KVH = 4
HD = 128
ALEN = 128
ANS_ROWS = 4096
PROMPT = 2048
N_ANS = 32


def shared_keys(key):
    return jax.random.normal(jax.random.fold_in(key, 11), (PROMPT, KVH, HD), jnp.float32)


def draw_q_ans(key, part):
    key = jax.random.fold_in(key, 5)
    base = jax.random.normal(key, (ANS_ROWS, HQ, HD), jnp.float32)
    return base.reshape(ANS_ROWS, HQ * HD).astype(jnp.bfloat16)


def draw_q_prompt(key, part):
    key = jax.random.fold_in(key, 6)
    base = jax.random.normal(key, (PROMPT, HQ, HD), jnp.float32)
    return base.reshape(PROMPT, HQ * HD).astype(jnp.bfloat16)


def draw_kv_prompt(key, part):
    keys = shared_keys(key)
    key = jax.random.fold_in(key, 3)
    values = jax.random.normal(key, (PROMPT, KVH, HD), jnp.float32)
    keys = jnp.clip(keys, -8.0, 8.0)
    return jnp.stack([keys.reshape(PROMPT, KVH * HD), values.reshape(PROMPT, KVH * HD)]).astype(jnp.bfloat16)


def draw_ans_len(key, part):
    key = jax.random.fold_in(key, 7)
    lengths = jax.random.randint(key, (N_ANS,), ALEN // 4, ALEN + 1)
    longest = jax.random.randint(jax.random.fold_in(key, 1), (), 0, N_ANS)
    return jnp.where(jnp.arange(N_ANS) == longest, ALEN, lengths).astype(jnp.int32)


def block_scale(key, extent, shards, low, largest):
    def one(position, shards_of):
        steps = jax.random.uniform(jax.random.fold_in(jax.random.fold_in(key, 6), position), (shards_of,), jnp.float32, low / len(shards), largest / len(shards))
        return jnp.repeat(jnp.exp(steps), extent[position] // shards_of).reshape((-1,) + (1,) * (len(extent) - position - 1))

    loudness = one(*shards[0])
    for cut in shards[1:]:
        loudness = loudness * one(*cut)
    return loudness


def bell_draw(key, extent, width, bound, split=(), kind=jnp.bfloat16):
    drawn = width * jax.random.normal(key, extent, jnp.float32)
    if split:
        drawn = drawn * block_scale(key, extent, split, -0.22, 0.18)
    return jnp.clip(drawn, -bound, bound).astype(kind)


def setup_inputs(seed: int = 0, part: int = 0) -> dict:
    seeds = jax.random.split(jax.random.key(seed), 9)
    part_splits = jax.random.split(jax.random.fold_in(seeds[8], part), 9)
    q_ans = draw_q_ans(jax.random.fold_in(jax.random.fold_in(seeds[8], part), 71), part)
    kv_ans = bell_draw(part_splits[1], (2, ANS_ROWS, KVH * HD), 1.0, 6.0, ((1, 32), (2, 4)))
    q_prompt = draw_q_prompt(jax.random.fold_in(jax.random.fold_in(seeds[8], part), 71), part)
    kv_prompt = draw_kv_prompt(jax.random.fold_in(jax.random.fold_in(seeds[8], part), 71), part)
    dout_ans = bell_draw(part_splits[4], (ANS_ROWS, HQ * HD), 8.0, 48.0, ((0, 32), (1, 4)))
    dout_prompt = bell_draw(part_splits[5], (PROMPT, HQ * HD), 8.0, 48.0, ((0, 32), (1, 4)))
    ans_len = draw_ans_len(jax.random.fold_in(jax.random.fold_in(seeds[8], part), 71), part)
    prompt_len = jax.random.randint(part_splits[7], (1,), PROMPT // 4, PROMPT + 1).astype(jnp.int32)
    return dict(q_ans=q_ans, kv_ans=kv_ans, q_prompt=q_prompt, kv_prompt=kv_prompt, dout_ans=dout_ans, dout_prompt=dout_prompt, ans_len=ans_len, prompt_len=prompt_len)


NEG_FILL = -1e+30

def scores_of(rows, keys, mask, scale):
    raw = jnp.einsum('nd,sd->ns', rows.astype(jnp.float32), keys.astype(jnp.float32)) * scale
    return jnp.where(mask, raw, NEG_FILL)

def block_pass(rows, grads_in, keys, values, mask, scale):
    score = scores_of(rows, keys, mask, scale)
    top = lax.optimization_barrier(jnp.max(score, axis=1, keepdims=True))
    expo = jnp.exp(score - top)
    total = lax.optimization_barrier(jnp.sum(expo, axis=1, keepdims=True))
    prob = expo / total
    prob_b = prob.astype(jnp.bfloat16)
    attended = jnp.dot(prob_b, values, preferred_element_type=jnp.float32)
    delta = lax.optimization_barrier(jnp.sum(grads_in.astype(jnp.float32) * attended, axis=1, keepdims=True))
    dprob = jnp.einsum('nd,sd->ns', grads_in.astype(jnp.float32), values.astype(jnp.float32))
    dscore = (prob * (dprob - delta) * scale).astype(jnp.bfloat16)
    dquery = jnp.dot(dscore, keys, preferred_element_type=jnp.float32)
    return (prob_b, dscore, dquery)

def key_grads(prob_b, dscore, rows, grads_in):
    dkey = jnp.einsum('ns,nd->sd', dscore.astype(jnp.float32), rows.astype(jnp.float32))
    dvalue = jnp.einsum('ns,nd->sd', prob_b.astype(jnp.float32), grads_in.astype(jnp.float32))
    return (dkey, dvalue)

def reference(q_ans, kv_ans, q_prompt, kv_prompt, dout_ans, dout_prompt, ans_len, prompt_len):
    group = HQ // KVH
    scale = 1.0 / math.sqrt(HD)
    plen = prompt_len[0]
    columns = jnp.arange(PROMPT)
    key_ok = columns < plen
    rows_n = ALEN * group
    token = jnp.arange(rows_n) // group
    own_ok = jnp.arange(ALEN)[None, :] <= token[:, None]
    prompt_pos = jnp.arange(PROMPT * group) // group
    prompt_mask = key_ok[None, :] & (columns[None, :] <= prompt_pos[:, None])
    dq_a, dk_a, dv_a, dq_p, dk_p, dv_p = ([], [], [], [], [], [])
    for head in range(KVH):
        qcols = slice(head * group * HD, (head + 1) * group * HD)
        kcols = slice(head * HD, (head + 1) * HD)
        keys_p = kv_prompt[0, :, kcols]
        vals_p = kv_prompt[1, :, kcols]
        q_head = q_ans[:, qcols]
        g_head = dout_ans[:, qcols]
        k_own_all = kv_ans[0, :, kcols]
        v_own_all = kv_ans[1, :, kcols]

        def one_answer(index):
            start = (index * ALEN).astype(jnp.int32)
            rows = lax.dynamic_slice_in_dim(q_head, start, ALEN, 0).reshape(rows_n, HD)
            grads_in = lax.dynamic_slice_in_dim(g_head, start, ALEN, 0).reshape(rows_n, HD)
            live = (token < ans_len[index])[:, None]
            grads_in = jnp.where(live, grads_in, jnp.zeros((), jnp.bfloat16))
            own_k = lax.dynamic_slice_in_dim(k_own_all, start, ALEN, 0)
            own_v = lax.dynamic_slice_in_dim(v_own_all, start, ALEN, 0)
            keys = jnp.concatenate([keys_p, own_k], 0)
            values = jnp.concatenate([vals_p, own_v], 0)
            mask = jnp.concatenate([jnp.broadcast_to(key_ok[None, :], (rows_n, PROMPT)), own_ok], 1)
            prob_b, dscore, dquery = block_pass(rows, grads_in, keys, values, mask, scale)
            dkey, dvalue = key_grads(prob_b, dscore, rows, grads_in)
            return (dquery.reshape(ALEN, group * HD).astype(jnp.bfloat16), dkey[PROMPT:], dvalue[PROMPT:], dkey[:PROMPT], dvalue[:PROMPT])
        dquery, dko, dvo, dkp, dvp = lax.map(one_answer, jnp.arange(N_ANS, dtype=jnp.int32))
        dq_a.append(dquery.reshape(ANS_ROWS, group * HD))
        dk_a.append(dko.reshape(ANS_ROWS, HD))
        dv_a.append(dvo.reshape(ANS_ROWS, HD))
        rows = q_prompt[:, qcols].reshape(PROMPT * group, HD)
        grads_in = dout_prompt[:, qcols].reshape(PROMPT * group, HD)
        grads_in = jnp.where((prompt_pos < plen)[:, None], grads_in, jnp.zeros((), jnp.bfloat16))
        prob_b, dscore, dquery_p = block_pass(rows, grads_in, keys_p, vals_p, prompt_mask, scale)
        dkey, dvalue = key_grads(prob_b, dscore, rows, grads_in)
        dq_p.append(dquery_p.reshape(PROMPT, group * HD).astype(jnp.bfloat16))
        dk_p.append(lax.optimization_barrier(jnp.sum(dkp, axis=0)) + dkey)
        dv_p.append(lax.optimization_barrier(jnp.sum(dvp, axis=0)) + dvalue)
    d_q_ans = jnp.concatenate(dq_a, 1)
    d_kv_ans = jnp.stack([jnp.concatenate(dk_a, 1), jnp.concatenate(dv_a, 1)]).astype(jnp.bfloat16)
    d_q_prompt = jnp.concatenate(dq_p, 1)
    d_kv_prompt = jnp.stack([jnp.concatenate(dk_p, 1), jnp.concatenate(dv_p, 1)]).astype(jnp.bfloat16)
    return (d_q_ans, d_kv_ans, d_q_prompt, d_kv_prompt)
```

```python
import functools
import math

import jax
import jax.numpy as jnp
from jax import lax
from jax.experimental import pallas as pl
from jax.experimental.pallas import tpu as pltpu
from jax.sharding import PartitionSpec as P

MESH = pl.DeviceIdType.MESH
F32, BF16 = jnp.float32, jnp.bfloat16
HD = 128
HEADS = 8
ALEN = 128
PIECE = 64
A_ROWS = HEADS * ALEN
P_ROWS = HEADS * PIECE
ROWS = A_ROWS + P_ROWS
LANES = 256
CHUNKS = ROWS // LANES
SCALE = 1.0 / math.sqrt(HD)
COEF = SCALE * math.log2(math.e)
NEG = -1e30
NT = (((1,), (1,)), ((), ()))


def kernel(nz, ans_len, prompt_len, q_a, kv_a, q_p, kv_p, g_a, g_p,
           dq_a, dkv_a, dq_p, dkv_p,
           kv, kt, q, g, e, dp, ds, pbuf, mrun, tot, mgrp, rgrp, delta,
           terms, dq, own_out, prm_out, rs_in, rs_out, x_in, x_out,
           ld_sem, st_sem, ag_send, ag_recv, gx_send, gx_recv,
           rs_send, rs_recv, rx_send, rx_recv):
    half = nz // 2
    me = lax.axis_index("ans")
    par = me // nz
    z = me % nz
    right = par * nz + (z + 1) % nz
    left = par * nz + (z + nz - 1) % nz
    cross = (1 - par) * nz + z
    alen = ans_len[0]
    plen = prompt_len[0]
    n_keys = 256 * half + 128

    def towards(d):
        return {"ans": right if d == 0 else left}

    for h in range(HEADS):
        cols = pl.ds(h * HD, HD)
        pltpu.make_async_copy(q_a.at[:, cols], q.at[pl.ds(h * ALEN, ALEN)], ld_sem.at[0]).start()
        pltpu.make_async_copy(q_p.at[:, cols], q.at[pl.ds(A_ROWS + h * PIECE, PIECE)], ld_sem.at[0]).start()
        pltpu.make_async_copy(g_a.at[:, cols], g.at[pl.ds(h * ALEN, ALEN)], ld_sem.at[1]).start()
        pltpu.make_async_copy(g_p.at[:, cols], g.at[pl.ds(A_ROWS + h * PIECE, PIECE)], ld_sem.at[1]).start()
    own_row = pl.multiple_of(par * PIECE, PIECE)
    cross_row = pl.multiple_of((1 - par) * PIECE, PIECE)
    own_load = pltpu.make_async_copy(kv_p, kv.at[:, pl.ds(own_row, PIECE)], ld_sem.at[2])
    own_load.start()
    ans_load = pltpu.make_async_copy(kv_a, kv.at[:, pl.ds(128, ALEN)], ld_sem.at[3])
    ans_load.start()

    barrier = pltpu.get_barrier_semaphore()
    for peer in (right, left, cross):
        pl.semaphore_signal(barrier, inc=1, device_id={"ans": peer}, device_id_type=MESH)
    pl.semaphore_wait(barrier, 3)

    def block_row(s, d, r):
        return pl.multiple_of(s * 256 + d * 128 + r * PIECE, PIECE)

    def hop(s, d, c, r, src=None):
        first = isinstance(s, int) and s == 1
        last = isinstance(s, int) and s == half
        if src is None:
            row = pl.multiple_of(r * PIECE, PIECE) if first else block_row(s - 1, d, r)
            src = kv.at[c, pl.ds(row, PIECE)]
        row = 256 * half + r * PIECE if last else block_row(s, d, r)
        return pltpu.make_async_remote_copy(
            src_ref=src, dst_ref=kv.at[c, pl.ds(row, PIECE)],
            send_sem=ag_send.at[d, c, r], recv_sem=ag_recv.at[s - 1, d, c, r],
            device_id=towards(d), device_id_type=MESH)

    def exchange(c):
        return pltpu.make_async_remote_copy(
            src_ref=kv_p.at[c], dst_ref=kv.at[c, pl.ds(own_row, PIECE)],
            send_sem=gx_send.at[c], recv_sem=gx_recv.at[c],
            device_id={"ans": cross}, device_id_type=MESH)

    def arrival(c):
        return pltpu.make_async_remote_copy(
            src_ref=kv_p.at[c], dst_ref=kv.at[c, pl.ds(cross_row, PIECE)],
            send_sem=gx_send.at[c], recv_sem=gx_recv.at[c],
            device_id={"ans": cross}, device_id_type=MESH)

    for c in range(2):
        exchange(c).start()
        for d in range(2):
            hop(1, d, c, par, kv_p.at[c]).start()
    for c in range(2):
        arrival(c).wait_recv()
        for d in range(2):
            hop(1, d, c, 1 - par).start()

    pltpu.make_async_copy(q, q, ld_sem.at[0]).wait()
    pltpu.make_async_copy(g, g, ld_sem.at[1]).wait()
    own_load.wait()
    ans_load.wait()
    tok = lax.broadcasted_iota(jnp.int32, (A_ROWS, HD), 0) & (ALEN - 1)
    g[0:A_ROWS] = jnp.where(tok < alen, g[0:A_ROWS], jnp.zeros((), BF16))
    tok = me * PIECE + (lax.broadcasted_iota(jnp.int32, (P_ROWS, HD), 0) & (PIECE - 1))
    g[A_ROWS:ROWS] = jnp.where(tok < plen, g[A_ROWS:ROWS], jnp.zeros((), BF16))

    def limits(j):
        lane = lax.broadcasted_iota(jnp.int32, (1, LANES), 1)
        if j * LANES < A_ROWS:
            return jnp.zeros((1, LANES), jnp.int32) + (plen - 1), lane & (ALEN - 1)
        pos = me * PIECE + (lane & (PIECE - 1))
        return jnp.minimum(pos, plen - 1), jnp.full((1, LANES), -1, jnp.int32)

    def score_group(s, off, bases, own):
        n = PIECE * len(bases) + (ALEN if own else 0)
        rows = pl.ds(off, n)
        keys = kv[0, rows, :]
        values = kv[1, rows, :]
        for j in range(CHUNKS):
            lanes = slice(j * LANES, (j + 1) * LANES)
            lim, lim_own = limits(j)
            raw = lax.dot_general(keys, q[lanes, :], NT, preferred_element_type=F32)
            parts = []
            for b, base in enumerate(bases):
                pos = base + lax.broadcasted_iota(jnp.int32, (PIECE, LANES), 0)
                parts.append(jnp.where(pos <= lim, raw[b * PIECE:(b + 1) * PIECE], NEG))
            if own:
                pos = lax.broadcasted_iota(jnp.int32, (ALEN, LANES), 0)
                parts.append(jnp.where(pos <= lim_own, raw[n - ALEN:n], NEG))
            raw = jnp.concatenate(parts, 0).reshape(n // 8, 8, LANES)
            high = jnp.max(raw, axis=0)
            if own:
                new = high
            else:
                old = mrun[:, lanes]
                new = jnp.maximum(old, high)
            ex = jnp.exp2((raw - new[None]) * COEF)
            part = jnp.sum(ex, axis=0)
            if own:
                tot[:, lanes] = part
            else:
                tot[:, lanes] = tot[:, lanes] * jnp.exp2((old - new) * COEF) + part
            mrun[:, lanes] = new
            mgrp[s, :, lanes] = new
            e[rows, lanes] = ex.reshape(n, LANES)
            dp[rows, lanes] = lax.dot_general(values, g[lanes, :], NT, preferred_element_type=F32)

    def base_of(s, d, r):
        there = (z + nz - s) % nz if d == 0 else (z + s) % nz
        return (r * nz + there) * PIECE

    score_group(0, 0, [base_of(0, 0, 0), base_of(0, 0, 1)], True)

    def middle(s, carry):
        for r in (par, 1 - par):
            for c in range(2):
                for d in range(2):
                    hop(s, d, c, r).wait()
                    hop(s + 1, d, c, r).start()
        score_group(s, pl.multiple_of(s * 256, 256),
                    [base_of(s, d, r) for d in range(2) for r in range(2)], False)
        return carry

    for r in (par, 1 - par):
        for c in range(2):
            for d in range(2):
                hop(1, d, c, r).wait()
                hop(2, d, c, r).start()
    score_group(1, 256, [base_of(1, d, r) for d in range(2) for r in range(2)], False)
    lax.fori_loop(2, half - 1, middle, 0)
    s = half - 1
    for r in range(2):
        for c in range(2):
            for d in range(2):
                hop(s, d, c, r).wait()
                if r == d:
                    hop(half, d, c, r).start()
    score_group(s, s * 256, [base_of(s, d, r) for d in range(2) for r in range(2)], False)
    for c in range(2):
        for d in range(2):
            hop(half, d, c, d).wait()
    for c in range(2):
        exchange(c).wait_send()
    score_group(half, half * 256, [base_of(half, d, d) for d in range(2)], False)

    m8 = mrun[...]
    top = jnp.max(m8, axis=0, keepdims=True)
    total = jnp.sum(tot[...] * jnp.exp2((m8 - top) * COEF), axis=0, keepdims=True)
    inv = 1.0 / total
    for s in range(half + 1):
        rgrp[s] = jnp.exp2((mgrp[s] - top) * COEF) * inv
    delta[...] = jnp.zeros_like(delta)

    def rows_of(s):
        return pl.multiple_of(s * 256, 256) if not isinstance(s, int) else s * 256

    def value_terms(s, n=256):
        rows = pl.ds(rows_of(s), n)
        for j in range(CHUNKS):
            lanes = slice(j * LANES, (j + 1) * LANES)
            p = e[rows, lanes].reshape(n // 8, 8, LANES) * rgrp[s, :, lanes][None]
            pb = p.reshape(n, LANES).astype(BF16)
            pbuf[0:n, lanes] = pb
            prod = pb.astype(F32) * dp[rows, lanes]
            delta[:, lanes] += jnp.sum(prod.reshape(n // 8, 8, LANES), axis=0)
        terms[1, rows, :] = jnp.dot(pbuf[0:n], g[...], preferred_element_type=F32)

    def key_terms(s, n=256):
        rows = pl.ds(rows_of(s), n)
        for j in range(CHUNKS):
            lanes = slice(j * LANES, (j + 1) * LANES)
            p = e[rows, lanes].reshape(n // 8, 8, LANES) * (rgrp[s, :, lanes] * SCALE)[None]
            diff = dp[rows, lanes].reshape(n // 8, 8, LANES) - delta[:, lanes][None]
            ds[rows, lanes] = (p * diff).reshape(n, LANES).astype(BF16)
        terms[0, rows, :] = jnp.dot(ds[rows, :], q[...], preferred_element_type=F32)

    def query_terms(j):
        lanes = slice(j * LANES, (j + 1) * LANES)
        flipped = jnp.dot(kt[...], ds[:, lanes], preferred_element_type=F32)
        dq[lanes, :] = flipped.T.astype(BF16)

    def run(fn, first, last):
        if first >= last:
            lax.fori_loop(0, first - last + 1, lambda i, carry: (fn(first - i), carry)[1], 0)

    def partial_sum(far, d, c, r):
        return pltpu.make_async_remote_copy(
            src_ref=rs_out.at[far - 1, d, c, r], dst_ref=rs_in.at[far - 1, d, c, r],
            send_sem=rs_send.at[d, c, r], recv_sem=rs_recv.at[far - 1, d, c, r],
            device_id=towards(d), device_id_type=MESH)

    def ring(c, far):
        for r in range(2):
            for d in range(2):
                if far == half:
                    if r != d:
                        continue
                    row = half * 256 + r * PIECE
                else:
                    row = far * 256 + (1 - d) * 128 + r * PIECE
                term = terms[c, row:row + PIECE, :]
                if far < half - 1 or (far == half - 1 and r == d):
                    partial_sum(far + 1, d, c, r).wait()
                    term = term + rs_in[far, d, c, r].astype(F32)
                rs_out[far - 1, d, c, r] = term.astype(BF16)
                partial_sum(far, d, c, r).start()

    def swap(c):
        return pltpu.make_async_remote_copy(
            src_ref=x_out.at[c], dst_ref=x_in.at[c],
            send_sem=rx_send.at[c], recv_sem=rx_recv.at[c],
            device_id={"ans": cross}, device_id_type=MESH)

    def gathered_sum(c, row, r):
        acc = terms[c, pl.ds(row, PIECE), :]
        for d in range(2):
            partial_sum(1, d, c, r).wait()
            acc = acc + rs_in[0, d, c, r].astype(F32)
        return acc

    def finish(c):
        x_out[c] = gathered_sum(c, cross_row, 1 - par).astype(BF16)
        swap(c).start()
        terms[c, pl.ds(own_row, PIECE), :] = gathered_sum(c, own_row, par)

    def settle(c):
        swap(c).wait()
        prm_out[c] = (terms[c, pl.ds(own_row, PIECE), :] + x_in[c].astype(F32)).astype(BF16)

    K, V = 0, 1
    value_terms(half, 128)
    ring(V, half)
    run(value_terms, half - 1, half // 2)
    ring(V, half - 1)
    run(value_terms, half // 2 - 1, 0)
    delta[...] = jnp.broadcast_to(jnp.sum(delta[...], axis=0, keepdims=True), delta.shape)
    key_terms(half, 128)
    ring(K, half)
    vnext = half - 2
    knext = half - 1
    ring(V, vnext)
    group = half - 1
    while group >= 0:
        low = max(group - 1, 0)
        run(key_terms, group, low)
        group = low - 1
        ring(K, knext)
        knext -= 1
        vnext -= 1
        if vnext >= 1:
            ring(V, vnext)
        elif vnext == 0:
            finish(V)
    own_out[...] = terms[:, 128:256, :].astype(BF16)
    for s in range(n_keys // 128):
        kt[:, s * 128:(s + 1) * 128] = kv[0, s * 128:(s + 1) * 128, :].T
    for j in range(CHUNKS):
        query_terms(j)
        if j % 2 == 1:
            if knext >= 1:
                ring(K, knext)
                knext -= 1
            vnext -= 1
            if vnext >= 1:
                ring(V, vnext)
            elif vnext == 0:
                finish(V)
    stores = [pltpu.make_async_copy(own_out, dkv_a, st_sem.at[0])]
    stores[0].start()
    for h in range(HEADS):
        cols = pl.ds(h * HD, HD)
        pltpu.make_async_copy(dq.at[pl.ds(h * ALEN, ALEN)], dq_a.at[:, cols], st_sem.at[1]).start()
        pltpu.make_async_copy(dq.at[pl.ds(A_ROWS + h * PIECE, PIECE)], dq_p.at[:, cols], st_sem.at[1]).start()
    while knext >= 1:
        ring(K, knext)
        knext -= 1
    finish(K)
    settle(V)
    settle(K)
    out = pltpu.make_async_copy(prm_out, dkv_p, st_sem.at[2])
    out.start()
    stores[0].wait()
    pltpu.make_async_copy(dq, dq, st_sem.at[1]).wait()
    out.wait()


def per_device(nz, q_ans, kv_ans, q_prompt, kv_prompt, dout_ans, dout_prompt, ans_len, prompt_len):
    half = nz // 2
    n_keys = 256 * half + 128
    any_spec = pl.BlockSpec(memory_space=pl.ANY)
    smem = pl.BlockSpec(memory_space=pltpu.SMEM)
    dma, vm = pltpu.SemaphoreType.DMA, pltpu.VMEM
    blocks = (half, 2, 2, 2)
    return pl.pallas_call(
        functools.partial(kernel, nz),
        out_shape=(
            jax.ShapeDtypeStruct(q_ans.shape, BF16),
            jax.ShapeDtypeStruct(kv_ans.shape, BF16),
            jax.ShapeDtypeStruct(q_prompt.shape, BF16),
            jax.ShapeDtypeStruct(kv_prompt.shape, BF16),
        ),
        in_specs=[smem, smem] + [any_spec] * 6,
        out_specs=(any_spec,) * 4,
        scratch_shapes=[
            vm((2, n_keys, HD), BF16),
            vm((HD, n_keys), BF16),
            vm((ROWS, HD), BF16),
            vm((ROWS, HD), BF16),
            vm((n_keys, ROWS), F32),
            vm((n_keys, ROWS), F32),
            vm((n_keys, ROWS), BF16),
            vm((256, ROWS), BF16),
            vm((8, ROWS), F32),
            vm((8, ROWS), F32),
            vm((half + 1, 8, ROWS), F32),
            vm((half + 1, 8, ROWS), F32),
            vm((8, ROWS), F32),
            vm((2, n_keys, HD), F32),
            vm((ROWS, HD), BF16),
            vm((2, ALEN, HD), BF16),
            vm((2, PIECE, HD), BF16),
            vm(blocks + (PIECE, HD), BF16),
            vm(blocks + (PIECE, HD), BF16),
            vm((2, PIECE, HD), BF16),
            vm((2, PIECE, HD), BF16),
            dma((4,)), dma((3,)),
            dma((2, 2, 2)), dma(blocks), dma((2,)), dma((2,)),
            dma((2, 2, 2)), dma(blocks), dma((2,)), dma((2,)),
        ],
        compiler_params=pltpu.CompilerParams(
            collective_id=0, has_side_effects=True, vmem_limit_bytes=58 * 1024 * 1024),
    )(ans_len, prompt_len, q_ans, kv_ans, q_prompt, kv_prompt, dout_ans, dout_prompt)


def solution(mesh):
    in_specs = (
        P(("group", "ans"), "tp"),
        P(None, ("group", "ans"), "tp"),
        P(("group", "ans"), "tp"),
        P(None, ("group", "ans"), "tp"),
        P(("group", "ans"), "tp"),
        P(("group", "ans"), "tp"),
        P(("group", "ans")),
        P("group"),
    )
    out_specs = (
        P(("group", "ans"), "tp"),
        P(None, ("group", "ans"), "tp"),
        P(("group", "ans"), "tp"),
        P(None, ("group", "ans"), "tp"),
    )
    return jax.shard_map(
        functools.partial(per_device, mesh.shape["ans"] // 2), mesh=mesh,
        in_specs=in_specs, out_specs=out_specs, check_vma=False)
```

```python
import functools
import math

import jax
import jax.numpy as jnp
from jax import lax
from jax.experimental import pallas as pl
from jax.experimental.pallas import tpu as pltpu
from jax.sharding import PartitionSpec as P

MESH = pl.DeviceIdType.MESH
F32, BF16 = jnp.float32, jnp.bfloat16
HD = 128
HEADS = 8
ALEN = 128
PIECE = 64
A_ROWS = HEADS * ALEN
P_ROWS = HEADS * PIECE
ROWS = A_ROWS + P_ROWS
LANES = 256
CHUNKS = ROWS // LANES
SCALE = 1.0 / math.sqrt(HD)
COEF = SCALE * math.log2(math.e)
NEG = -1e30
NT = (((1,), (1,)), ((), ()))


def gather(nz, kv_p, kv_out, kv, ld_sem, ag_send, ag_recv, gx_send, gx_recv):
    half = nz // 2
    me = lax.axis_index("ans")
    par = me // nz
    z = me % nz
    own_load = pltpu.make_async_copy(kv_p, kv.at[:, pl.ds(pl.multiple_of(par * PIECE, PIECE), PIECE)], ld_sem.at[0])
    own_load.start()
    right = par * nz + (z + 1) % nz
    left = par * nz + (z + nz - 1) % nz
    cross = (1 - par) * nz + z
    own_row = pl.multiple_of(par * PIECE, PIECE)
    cross_row = pl.multiple_of((1 - par) * PIECE, PIECE)

    def towards(d):
        return {"ans": right if d == 0 else left}

    barrier = pltpu.get_barrier_semaphore()
    for peer in (right, left, cross):
        pl.semaphore_signal(barrier, inc=1, device_id={"ans": peer}, device_id_type=MESH)
    pl.semaphore_wait(barrier, 3)

    def block_row(s, d, r):
        return pl.multiple_of(s * 256 + d * 128 + r * PIECE, PIECE)

    def hop(s, d, c, r, src=None):
        first = isinstance(s, int) and s == 1
        last = isinstance(s, int) and s == half
        if src is None:
            row = pl.multiple_of(r * PIECE, PIECE) if first else block_row(s - 1, d, r)
            src = kv.at[c, pl.ds(row, PIECE)]
        row = 256 * half + r * PIECE if last else block_row(s, d, r)
        return pltpu.make_async_remote_copy(
            src_ref=src, dst_ref=kv.at[c, pl.ds(row, PIECE)],
            send_sem=ag_send.at[d, c, r], recv_sem=ag_recv.at[s - 1, d, c, r],
            device_id=towards(d), device_id_type=MESH)

    def exchange(c):
        return pltpu.make_async_remote_copy(
            src_ref=kv_p.at[c], dst_ref=kv.at[c, pl.ds(own_row, PIECE)],
            send_sem=gx_send.at[c], recv_sem=gx_recv.at[c],
            device_id={"ans": cross}, device_id_type=MESH)

    def arrival(c):
        return pltpu.make_async_remote_copy(
            src_ref=kv_p.at[c], dst_ref=kv.at[c, pl.ds(cross_row, PIECE)],
            send_sem=gx_send.at[c], recv_sem=gx_recv.at[c],
            device_id={"ans": cross}, device_id_type=MESH)

    for c in range(2):
        exchange(c).start()
        for d in range(2):
            hop(1, d, c, par, kv_p.at[c]).start()
    for c in range(2):
        arrival(c).wait_recv()
        for d in range(2):
            hop(1, d, c, 1 - par).start()

    own_load.wait()

    def middle(s, carry):
        for r in (par, 1 - par):
            for c in range(2):
                for d in range(2):
                    hop(s, d, c, r).wait()
                    hop(s + 1, d, c, r).start()
        return carry

    for r in (par, 1 - par):
        for c in range(2):
            for d in range(2):
                hop(1, d, c, r).wait()
                hop(2, d, c, r).start()
    lax.fori_loop(2, half - 1, middle, 0)
    s = half - 1
    for r in range(2):
        for c in range(2):
            for d in range(2):
                hop(s, d, c, r).wait()
                if r == d:
                    hop(half, d, c, r).start()
    for c in range(2):
        for d in range(2):
            hop(half, d, c, d).wait()
    for c in range(2):
        exchange(c).wait_send()
    out = pltpu.make_async_copy(kv, kv_out, ld_sem.at[0])
    out.start()
    out.wait()


def attend(nz, ans_len, prompt_len, q_a, kv_a, q_p, kv_all, g_a, g_p,
           dq_a, dkv_a, dq_p, terms_out,
           kv, kt, q, g, e, dp, ds, pbuf, mrun, tot, mgrp, rgrp, delta,
           terms, dq, own_out, ld_sem, st_sem):
    half = nz // 2
    me = lax.axis_index("ans")
    par = me // nz
    z = me % nz
    alen = ans_len[0]
    plen = prompt_len[0]
    n_keys = 256 * half + 128
    for h in range(HEADS):
        cols = pl.ds(h * HD, HD)
        pltpu.make_async_copy(q_a.at[:, cols], q.at[pl.ds(h * ALEN, ALEN)], ld_sem.at[0]).start()
        pltpu.make_async_copy(q_p.at[:, cols], q.at[pl.ds(A_ROWS + h * PIECE, PIECE)], ld_sem.at[0]).start()
        pltpu.make_async_copy(g_a.at[:, cols], g.at[pl.ds(h * ALEN, ALEN)], ld_sem.at[1]).start()
        pltpu.make_async_copy(g_p.at[:, cols], g.at[pl.ds(A_ROWS + h * PIECE, PIECE)], ld_sem.at[1]).start()
    loads = [pltpu.make_async_copy(kv_all.at[:, pl.ds(0, 128)], kv.at[:, pl.ds(0, 128)], ld_sem.at[2]),
             pltpu.make_async_copy(kv_all.at[:, pl.ds(256, n_keys - 256)], kv.at[:, pl.ds(256, n_keys - 256)], ld_sem.at[3]),
             pltpu.make_async_copy(kv_a, kv.at[:, pl.ds(128, ALEN)], ld_sem.at[4])]
    for load in loads:
        load.start()
    for load in loads:
        load.wait()
    pltpu.make_async_copy(q, q, ld_sem.at[0]).wait()
    pltpu.make_async_copy(g, g, ld_sem.at[1]).wait()
    tok = lax.broadcasted_iota(jnp.int32, (A_ROWS, HD), 0) & (ALEN - 1)
    g[0:A_ROWS] = jnp.where(tok < alen, g[0:A_ROWS], jnp.zeros((), BF16))
    tok = me * PIECE + (lax.broadcasted_iota(jnp.int32, (P_ROWS, HD), 0) & (PIECE - 1))
    g[A_ROWS:ROWS] = jnp.where(tok < plen, g[A_ROWS:ROWS], jnp.zeros((), BF16))

    def limits(j):
        lane = lax.broadcasted_iota(jnp.int32, (1, LANES), 1)
        if j * LANES < A_ROWS:
            return jnp.zeros((1, LANES), jnp.int32) + (plen - 1), lane & (ALEN - 1)
        pos = me * PIECE + (lane & (PIECE - 1))
        return jnp.minimum(pos, plen - 1), jnp.full((1, LANES), -1, jnp.int32)

    def score_group(s, off, bases, own):
        n = PIECE * len(bases) + (ALEN if own else 0)
        rows = pl.ds(off, n)
        keys = kv[0, rows, :]
        values = kv[1, rows, :]
        for j in range(CHUNKS):
            lanes = slice(j * LANES, (j + 1) * LANES)
            lim, lim_own = limits(j)
            raw = lax.dot_general(keys, q[lanes, :], NT, preferred_element_type=F32)
            parts = []
            for b, base in enumerate(bases):
                pos = base + lax.broadcasted_iota(jnp.int32, (PIECE, LANES), 0)
                parts.append(jnp.where(pos <= lim, raw[b * PIECE:(b + 1) * PIECE], NEG))
            if own:
                pos = lax.broadcasted_iota(jnp.int32, (ALEN, LANES), 0)
                parts.append(jnp.where(pos <= lim_own, raw[n - ALEN:n], NEG))
            raw = jnp.concatenate(parts, 0).reshape(n // 8, 8, LANES)
            high = jnp.max(raw, axis=0)
            if own:
                new = high
            else:
                old = mrun[:, lanes]
                new = jnp.maximum(old, high)
            ex = jnp.exp2((raw - new[None]) * COEF)
            part = jnp.sum(ex, axis=0)
            if own:
                tot[:, lanes] = part
            else:
                tot[:, lanes] = tot[:, lanes] * jnp.exp2((old - new) * COEF) + part
            mrun[:, lanes] = new
            mgrp[s, :, lanes] = new
            e[rows, lanes] = ex.reshape(n, LANES)
            dp[rows, lanes] = lax.dot_general(values, g[lanes, :], NT, preferred_element_type=F32)

    def base_of(s, d, r):
        there = (z + nz - s) % nz if d == 0 else (z + s) % nz
        return (r * nz + there) * PIECE

    def four(s):
        return [base_of(s, d, r) for d in range(2) for r in range(2)]

    score_group(0, 0, [base_of(0, 0, 0), base_of(0, 0, 1)], True)

    def middle(s, carry):
        score_group(s, pl.multiple_of(s * 256, 256), four(s), False)
        return carry

    lax.fori_loop(1, half, middle, 0)
    score_group(half, half * 256, [base_of(half, d, d) for d in range(2)], False)

    m8 = mrun[...]
    top = jnp.max(m8, axis=0, keepdims=True)
    total = jnp.sum(tot[...] * jnp.exp2((m8 - top) * COEF), axis=0, keepdims=True)
    inv = 1.0 / total
    for s in range(half + 1):
        rgrp[s] = jnp.exp2((mgrp[s] - top) * COEF) * inv
    delta[...] = jnp.zeros_like(delta)

    def rows_of(s):
        return pl.multiple_of(s * 256, 256) if not isinstance(s, int) else s * 256

    def value_terms(s, n=256):
        rows = pl.ds(rows_of(s), n)
        for j in range(CHUNKS):
            lanes = slice(j * LANES, (j + 1) * LANES)
            p = e[rows, lanes].reshape(n // 8, 8, LANES) * rgrp[s, :, lanes][None]
            pb = p.reshape(n, LANES).astype(BF16)
            pbuf[0:n, lanes] = pb
            prod = pb.astype(F32) * dp[rows, lanes]
            delta[:, lanes] += jnp.sum(prod.reshape(n // 8, 8, LANES), axis=0)
        terms[1, rows, :] = jnp.dot(pbuf[0:n], g[...], preferred_element_type=F32)

    def key_terms(s, n=256):
        rows = pl.ds(rows_of(s), n)
        for j in range(CHUNKS):
            lanes = slice(j * LANES, (j + 1) * LANES)
            p = e[rows, lanes].reshape(n // 8, 8, LANES) * (rgrp[s, :, lanes] * SCALE)[None]
            diff = dp[rows, lanes].reshape(n // 8, 8, LANES) - delta[:, lanes][None]
            ds[rows, lanes] = (p * diff).reshape(n, LANES).astype(BF16)
        terms[0, rows, :] = jnp.dot(ds[rows, :], q[...], preferred_element_type=F32)

    def query_terms(j):
        lanes = slice(j * LANES, (j + 1) * LANES)
        flipped = jnp.dot(kt[...], ds[:, lanes], preferred_element_type=F32)
        dq[lanes, :] = flipped.T.astype(BF16)

    value_terms(half, 128)
    lax.fori_loop(0, half, lambda s, carry: (value_terms(s), carry)[1], 0)
    delta[...] = jnp.broadcast_to(jnp.sum(delta[...], axis=0, keepdims=True), delta.shape)
    key_terms(half, 128)
    lax.fori_loop(0, half, lambda s, carry: (key_terms(s), carry)[1], 0)
    sums = pltpu.make_async_copy(terms, terms_out, st_sem.at[2])
    sums.start()
    own_out[...] = terms[:, 128:256, :].astype(BF16)
    own = pltpu.make_async_copy(own_out, dkv_a, st_sem.at[0])
    own.start()
    for s in range(n_keys // 128):
        kt[:, s * 128:(s + 1) * 128] = kv[0, s * 128:(s + 1) * 128, :].T
    for j in range(CHUNKS):
        query_terms(j)
    for h in range(HEADS):
        cols = pl.ds(h * HD, HD)
        pltpu.make_async_copy(dq.at[pl.ds(h * ALEN, ALEN)], dq_a.at[:, cols], st_sem.at[1]).start()
        pltpu.make_async_copy(dq.at[pl.ds(A_ROWS + h * PIECE, PIECE)], dq_p.at[:, cols], st_sem.at[1]).start()
    sums.wait()
    own.wait()
    pltpu.make_async_copy(dq, dq, st_sem.at[1]).wait()


def scatter(nz, terms_in, dkv_p, terms, prm_out, rs_in, rs_out, x_in, x_out,
            ld_sem, rs_send, rs_recv, rx_send, rx_recv):
    half = nz // 2
    me = lax.axis_index("ans")
    par = me // nz
    z = me % nz
    load = pltpu.make_async_copy(terms_in, terms, ld_sem.at[0])
    load.start()
    right = par * nz + (z + 1) % nz
    left = par * nz + (z + nz - 1) % nz
    cross = (1 - par) * nz + z
    own_row = pl.multiple_of(par * PIECE, PIECE)
    cross_row = pl.multiple_of((1 - par) * PIECE, PIECE)

    def towards(d):
        return {"ans": right if d == 0 else left}

    barrier = pltpu.get_barrier_semaphore()
    for peer in (right, left, cross):
        pl.semaphore_signal(barrier, inc=1, device_id={"ans": peer}, device_id_type=MESH)
    pl.semaphore_wait(barrier, 3)

    def partial_sum(far, d, c, r):
        return pltpu.make_async_remote_copy(
            src_ref=rs_out.at[far - 1, d, c, r], dst_ref=rs_in.at[far - 1, d, c, r],
            send_sem=rs_send.at[d, c, r], recv_sem=rs_recv.at[far - 1, d, c, r],
            device_id=towards(d), device_id_type=MESH)

    def ring(c, far):
        for r in range(2):
            for d in range(2):
                if far == half:
                    if r != d:
                        continue
                    row = half * 256 + r * PIECE
                else:
                    row = far * 256 + (1 - d) * 128 + r * PIECE
                term = terms[c, row:row + PIECE, :]
                if far < half - 1 or (far == half - 1 and r == d):
                    partial_sum(far + 1, d, c, r).wait()
                    term = term + rs_in[far, d, c, r].astype(F32)
                rs_out[far - 1, d, c, r] = term.astype(BF16)
                partial_sum(far, d, c, r).start()

    def swap(c):
        return pltpu.make_async_remote_copy(
            src_ref=x_out.at[c], dst_ref=x_in.at[c],
            send_sem=rx_send.at[c], recv_sem=rx_recv.at[c],
            device_id={"ans": cross}, device_id_type=MESH)

    def gathered_sum(c, row, r):
        acc = terms[c, pl.ds(row, PIECE), :]
        for d in range(2):
            partial_sum(1, d, c, r).wait()
            acc = acc + rs_in[0, d, c, r].astype(F32)
        return acc

    def finish(c):
        x_out[c] = gathered_sum(c, cross_row, 1 - par).astype(BF16)
        swap(c).start()
        terms[c, pl.ds(own_row, PIECE), :] = gathered_sum(c, own_row, par)

    def settle(c):
        swap(c).wait()
        prm_out[c] = (terms[c, pl.ds(own_row, PIECE), :] + x_in[c].astype(F32)).astype(BF16)

    load.wait()
    for far in range(half, 0, -1):
        ring(1, far)
        ring(0, far)
    finish(1)
    finish(0)
    settle(1)
    settle(0)
    out = pltpu.make_async_copy(prm_out, dkv_p, ld_sem.at[0])
    out.start()
    out.wait()


def per_device(nz, q_ans, kv_ans, q_prompt, kv_prompt, dout_ans, dout_prompt, ans_len, prompt_len):
    half = nz // 2
    n_keys = 256 * half + 128
    any_spec = pl.BlockSpec(memory_space=pl.ANY)
    smem = pl.BlockSpec(memory_space=pltpu.SMEM)
    dma, vm = pltpu.SemaphoreType.DMA, pltpu.VMEM
    blocks = (half, 2, 2, 2)
    gathered = pl.pallas_call(
        functools.partial(gather, nz),
        out_shape=jax.ShapeDtypeStruct((2, n_keys, HD), BF16),
        in_specs=[any_spec],
        out_specs=any_spec,
        scratch_shapes=[
            vm((2, n_keys, HD), BF16), dma((1,)),
            dma((2, 2, 2)), dma(blocks), dma((2,)), dma((2,)),
        ],
        compiler_params=pltpu.CompilerParams(
            collective_id=0, has_side_effects=True, vmem_limit_bytes=58 * 1024 * 1024),
    )(kv_prompt)
    d_q_ans, d_kv_ans, d_q_prompt, terms = pl.pallas_call(
        functools.partial(attend, nz),
        out_shape=(
            jax.ShapeDtypeStruct(q_ans.shape, BF16),
            jax.ShapeDtypeStruct(kv_ans.shape, BF16),
            jax.ShapeDtypeStruct(q_prompt.shape, BF16),
            jax.ShapeDtypeStruct((2, n_keys, HD), F32),
        ),
        in_specs=[smem, smem] + [any_spec] * 6,
        out_specs=(any_spec,) * 4,
        scratch_shapes=[
            vm((2, n_keys, HD), BF16),
            vm((HD, n_keys), BF16),
            vm((ROWS, HD), BF16),
            vm((ROWS, HD), BF16),
            vm((n_keys, ROWS), F32),
            vm((n_keys, ROWS), F32),
            vm((n_keys, ROWS), BF16),
            vm((256, ROWS), BF16),
            vm((8, ROWS), F32),
            vm((8, ROWS), F32),
            vm((half + 1, 8, ROWS), F32),
            vm((half + 1, 8, ROWS), F32),
            vm((8, ROWS), F32),
            vm((2, n_keys, HD), F32),
            vm((ROWS, HD), BF16),
            vm((2, ALEN, HD), BF16),
            dma((5,)), dma((3,)),
        ],
        compiler_params=pltpu.CompilerParams(vmem_limit_bytes=58 * 1024 * 1024),
    )(ans_len, prompt_len, q_ans, kv_ans, q_prompt, gathered, dout_ans, dout_prompt)
    d_kv_prompt = pl.pallas_call(
        functools.partial(scatter, nz),
        out_shape=jax.ShapeDtypeStruct(kv_prompt.shape, BF16),
        in_specs=[any_spec],
        out_specs=any_spec,
        scratch_shapes=[
            vm((2, n_keys, HD), F32),
            vm((2, PIECE, HD), BF16),
            vm(blocks + (PIECE, HD), BF16),
            vm(blocks + (PIECE, HD), BF16),
            vm((2, PIECE, HD), BF16),
            vm((2, PIECE, HD), BF16),
            dma((1,)),
            dma((2, 2, 2)), dma(blocks), dma((2,)), dma((2,)),
        ],
        compiler_params=pltpu.CompilerParams(
            collective_id=1, has_side_effects=True, vmem_limit_bytes=58 * 1024 * 1024),
    )(terms)
    return d_q_ans, d_kv_ans, d_q_prompt, d_kv_prompt


def solution(mesh):
    in_specs = (
        P(("group", "ans"), "tp"),
        P(None, ("group", "ans"), "tp"),
        P(("group", "ans"), "tp"),
        P(None, ("group", "ans"), "tp"),
        P(("group", "ans"), "tp"),
        P(("group", "ans"), "tp"),
        P(("group", "ans")),
        P("group"),
    )
    out_specs = (
        P(("group", "ans"), "tp"),
        P(None, ("group", "ans"), "tp"),
        P(("group", "ans"), "tp"),
        P(None, ("group", "ans"), "tp"),
    )
    return jax.shard_map(
        functools.partial(per_device, mesh.shape["ans"] // 2), mesh=mesh,
        in_specs=in_specs, out_specs=out_specs, check_vma=False)
```

```python
import functools
import math

import jax
import jax.numpy as jnp
from jax import lax
from jax.experimental import pallas as pl
from jax.experimental.pallas import tpu as pltpu
from jax.sharding import PartitionSpec as P

MESH = pl.DeviceIdType.MESH
F32, BF16 = jnp.float32, jnp.bfloat16
HD = 128
HEADS = 8
ALEN = 128
PIECE = 64
A_ROWS = HEADS * ALEN
P_ROWS = HEADS * PIECE
ROWS = A_ROWS + P_ROWS
LANES = 256
CHUNKS = ROWS // LANES
SCALE = 1.0 / math.sqrt(HD)
COEF = SCALE * math.log2(math.e)
NEG = -1e30
NT = (((1,), (1,)), ((), ()))


def kernel(nz, ans_len, prompt_len, q_a, kv_a, q_p, kv_p, g_a, g_p,
           dq_a, dkv_a, dq_p, dkv_p,
           kv, kt, q, g, e, dp, ds, pbuf, mrun, tot, mgrp, rgrp, delta,
           terms, dq, own_out, prm_out, rs_in, rs_out, x_in, x_out,
           ld_sem, st_sem, ag_send, ag_recv, gx_send, gx_recv,
           rs_send, rs_recv, rx_send, rx_recv):
    half = nz // 2
    me = lax.axis_index("ans")
    par = me // nz
    z = me % nz
    right = par * nz + (z + 1) % nz
    left = par * nz + (z + nz - 1) % nz
    cross = (1 - par) * nz + z
    alen = ans_len[0]
    plen = prompt_len[0]
    n_keys = 256 * half + 128

    def towards(d):
        return {"ans": right if d == 0 else left}

    for h in range(HEADS):
        cols = pl.ds(h * HD, HD)
        pltpu.make_async_copy(q_a.at[:, cols], q.at[pl.ds(h * ALEN, ALEN)], ld_sem.at[0]).start()
        pltpu.make_async_copy(q_p.at[:, cols], q.at[pl.ds(A_ROWS + h * PIECE, PIECE)], ld_sem.at[0]).start()
        pltpu.make_async_copy(g_a.at[:, cols], g.at[pl.ds(h * ALEN, ALEN)], ld_sem.at[1]).start()
        pltpu.make_async_copy(g_p.at[:, cols], g.at[pl.ds(A_ROWS + h * PIECE, PIECE)], ld_sem.at[1]).start()
    own_row = pl.multiple_of(par * PIECE, PIECE)
    cross_row = pl.multiple_of((1 - par) * PIECE, PIECE)
    loads = [pltpu.make_async_copy(kv_p, kv.at[par], ld_sem.at[2])]
    for i in range(2):
        rows = pl.ds(i * PIECE, PIECE)
        loads.append(pltpu.make_async_copy(kv_a.at[:, rows], kv.at[2 + i], ld_sem.at[3 + i]))
    for load in loads:
        load.start()

    barrier = pltpu.get_barrier_semaphore()
    for peer in (right, left, cross):
        pl.semaphore_signal(barrier, inc=1, device_id={"ans": peer}, device_id_type=MESH)
    pl.semaphore_wait(barrier, 3)

    def hop(s, d, r, src=None):
        first = isinstance(s, int) and s == 1
        last = isinstance(s, int) and s == half
        if src is None:
            src = kv.at[r if first else 4 * (s - 1) + 2 * d + r]
        return pltpu.make_async_remote_copy(
            src_ref=src, dst_ref=kv.at[4 * half + r if last else 4 * s + 2 * d + r],
            send_sem=ag_send.at[d, r], recv_sem=ag_recv.at[s - 1, d, r],
            device_id=towards(d), device_id_type=MESH)

    def exchange(slot):
        return pltpu.make_async_remote_copy(
            src_ref=kv_p, dst_ref=kv.at[slot], send_sem=gx_send, recv_sem=gx_recv,
            device_id={"ans": cross}, device_id_type=MESH)

    exchange(par).start()
    for d in range(2):
        hop(1, d, par, kv_p).start()
    exchange(1 - par).wait_recv()
    for d in range(2):
        hop(1, d, 1 - par).start()

    pltpu.make_async_copy(q, q, ld_sem.at[0]).wait()
    pltpu.make_async_copy(g, g, ld_sem.at[1]).wait()
    for load in loads:
        load.wait()
    tok = lax.broadcasted_iota(jnp.int32, (A_ROWS, HD), 0) & (ALEN - 1)
    g[0:A_ROWS] = jnp.where(tok < alen, g[0:A_ROWS], jnp.zeros((), BF16))
    tok = me * PIECE + (lax.broadcasted_iota(jnp.int32, (P_ROWS, HD), 0) & (PIECE - 1))
    g[A_ROWS:ROWS] = jnp.where(tok < plen, g[A_ROWS:ROWS], jnp.zeros((), BF16))

    def limits(j):
        lane = lax.broadcasted_iota(jnp.int32, (1, LANES), 1)
        if j * LANES < A_ROWS:
            return jnp.zeros((1, LANES), jnp.int32) + (plen - 1), lane & (ALEN - 1)
        pos = me * PIECE + (lane & (PIECE - 1))
        return jnp.minimum(pos, plen - 1), jnp.full((1, LANES), -1, jnp.int32)

    def score_group(s, off, bases, own):
        n = PIECE * len(bases) + (ALEN if own else 0)
        rows = pl.ds(off, n)
        slots = pl.ds(4 * s, n // PIECE)
        keys = kv[slots, 0].reshape(n, HD)
        values = kv[slots, 1].reshape(n, HD)
        for j in range(CHUNKS):
            lanes = slice(j * LANES, (j + 1) * LANES)
            lim, lim_own = limits(j)
            raw = lax.dot_general(keys, q[lanes, :], NT, preferred_element_type=F32)
            parts = []
            for b, base in enumerate(bases):
                pos = base + lax.broadcasted_iota(jnp.int32, (PIECE, LANES), 0)
                parts.append(jnp.where(pos <= lim, raw[b * PIECE:(b + 1) * PIECE], NEG))
            if own:
                pos = lax.broadcasted_iota(jnp.int32, (ALEN, LANES), 0)
                parts.append(jnp.where(pos <= lim_own, raw[n - ALEN:n], NEG))
            raw = jnp.concatenate(parts, 0).reshape(n // 8, 8, LANES)
            high = jnp.max(raw, axis=0)
            if own:
                new = high
            else:
                old = mrun[:, lanes]
                new = jnp.maximum(old, high)
            ex = jnp.exp2((raw - new[None]) * COEF)
            part = jnp.sum(ex, axis=0)
            if own:
                tot[:, lanes] = part
            else:
                tot[:, lanes] = tot[:, lanes] * jnp.exp2((old - new) * COEF) + part
            mrun[:, lanes] = new
            mgrp[s, :, lanes] = new
            e[rows, lanes] = ex.reshape(n, LANES)
            dp[rows, lanes] = lax.dot_general(values, g[lanes, :], NT, preferred_element_type=F32)

    def base_of(s, d, r):
        there = (z + nz - s) % nz if d == 0 else (z + s) % nz
        return (r * nz + there) * PIECE

    score_group(0, 0, [base_of(0, 0, 0), base_of(0, 0, 1)], True)

    def pass_on(s):
        for r in (par, 1 - par):
            for d in range(2):
                hop(s, d, r).wait()
                hop(s + 1, d, r).start()

    def four(s):
        return [base_of(s, d, r) for d in range(2) for r in range(2)]

    def middle(s, carry):
        pass_on(s)
        score_group(s, pl.multiple_of(s * 256, 256), four(s), False)
        return carry

    pass_on(1)
    score_group(1, 256, four(1), False)
    lax.fori_loop(2, half - 1, middle, 0)
    s = half - 1
    for r in range(2):
        for d in range(2):
            hop(s, d, r).wait()
            if r == d:
                hop(half, d, r).start()
    score_group(s, s * 256, four(s), False)
    for d in range(2):
        hop(half, d, d).wait()
    exchange(par).wait_send()
    score_group(half, half * 256, [base_of(half, d, d) for d in range(2)], False)

    m8 = mrun[...]
    top = jnp.max(m8, axis=0, keepdims=True)
    total = jnp.sum(tot[...] * jnp.exp2((m8 - top) * COEF), axis=0, keepdims=True)
    inv = 1.0 / total
    for s in range(half + 1):
        rgrp[s] = jnp.exp2((mgrp[s] - top) * COEF) * inv
    delta[...] = jnp.zeros_like(delta)

    def rows_of(s):
        return pl.multiple_of(s * 256, 256) if not isinstance(s, int) else s * 256

    def value_terms(s, n=256):
        rows = pl.ds(rows_of(s), n)
        for j in range(CHUNKS):
            lanes = slice(j * LANES, (j + 1) * LANES)
            p = e[rows, lanes].reshape(n // 8, 8, LANES) * rgrp[s, :, lanes][None]
            pb = p.reshape(n, LANES).astype(BF16)
            pbuf[0:n, lanes] = pb
            prod = pb.astype(F32) * dp[rows, lanes]
            delta[:, lanes] += jnp.sum(prod.reshape(n // 8, 8, LANES), axis=0)
        terms[1, rows, :] = jnp.dot(pbuf[0:n], g[...], preferred_element_type=F32)

    def key_terms(s, n=256):
        rows = pl.ds(rows_of(s), n)
        for j in range(CHUNKS):
            lanes = slice(j * LANES, (j + 1) * LANES)
            p = e[rows, lanes].reshape(n // 8, 8, LANES) * (rgrp[s, :, lanes] * SCALE)[None]
            diff = dp[rows, lanes].reshape(n // 8, 8, LANES) - delta[:, lanes][None]
            ds[rows, lanes] = (p * diff).reshape(n, LANES).astype(BF16)
        terms[0, rows, :] = jnp.dot(ds[rows, :], q[...], preferred_element_type=F32)

    def query_terms(j):
        lanes = slice(j * LANES, (j + 1) * LANES)
        flipped = jnp.dot(kt[...], ds[:, lanes], preferred_element_type=F32)
        dq[lanes, :] = flipped.T.astype(BF16)

    def run(fn, first, last):
        if first >= last:
            lax.fori_loop(0, first - last + 1, lambda i, carry: (fn(first - i), carry)[1], 0)

    def partial_sum(far, d, c):
        part = pl.ds(d, 1) if far == half else pl.ds(0, 2)
        return pltpu.make_async_remote_copy(
            src_ref=rs_out.at[far - 1, d, c, part], dst_ref=rs_in.at[far - 1, d, c, part],
            send_sem=rs_send.at[d, c], recv_sem=rs_recv.at[far - 1, d, c],
            device_id=towards(d), device_id_type=MESH)

    def ring(c, far):
        for d in range(2):
            if far < half:
                partial_sum(far + 1, d, c).wait()
            for r in range(2):
                if far == half:
                    if r != d:
                        continue
                    row = half * 256 + r * PIECE
                else:
                    row = far * 256 + (1 - d) * 128 + r * PIECE
                term = terms[c, row:row + PIECE, :]
                if far < half - 1 or (far == half - 1 and r == d):
                    term = term + rs_in[far, d, c, r].astype(F32)
                rs_out[far - 1, d, c, r] = term.astype(BF16)
            partial_sum(far, d, c).start()

    def swap(c):
        return pltpu.make_async_remote_copy(
            src_ref=x_out.at[c], dst_ref=x_in.at[c],
            send_sem=rx_send.at[c], recv_sem=rx_recv.at[c],
            device_id={"ans": cross}, device_id_type=MESH)

    def gathered_sum(c, row, r):
        acc = terms[c, pl.ds(row, PIECE), :]
        for d in range(2):
            acc = acc + rs_in[0, d, c, r].astype(F32)
        return acc

    def finish(c):
        for d in range(2):
            partial_sum(1, d, c).wait()
        x_out[c] = gathered_sum(c, cross_row, 1 - par).astype(BF16)
        swap(c).start()
        terms[c, pl.ds(own_row, PIECE), :] = gathered_sum(c, own_row, par)

    def settle(c):
        swap(c).wait()
        prm_out[c] = (terms[c, pl.ds(own_row, PIECE), :] + x_in[c].astype(F32)).astype(BF16)

    K, V = 0, 1
    value_terms(half, 128)
    ring(V, half)
    run(value_terms, half - 1, half // 2)
    ring(V, half - 1)
    run(value_terms, half // 2 - 1, 0)
    delta[...] = jnp.broadcast_to(jnp.sum(delta[...], axis=0, keepdims=True), delta.shape)
    key_terms(half, 128)
    ring(K, half)
    vnext = half - 2
    knext = half - 1
    ring(V, vnext)
    group = half - 1
    while group >= 0:
        low = max(group - 1, 0)
        run(key_terms, group, low)
        group = low - 1
        ring(K, knext)
        knext -= 1
        vnext -= 1
        if vnext >= 1:
            ring(V, vnext)
        elif vnext == 0:
            finish(V)
    own_out[...] = terms[:, 128:256, :].astype(BF16)
    for s in range(n_keys // 128):
        kt[:, s * 128:(s + 1) * 128] = kv[2 * s:2 * s + 2, 0].reshape(128, HD).T
    for j in range(CHUNKS):
        query_terms(j)
        if j % 2 == 1:
            if knext >= 1:
                ring(K, knext)
                knext -= 1
            vnext -= 1
            if vnext >= 1:
                ring(V, vnext)
            elif vnext == 0:
                finish(V)
    stores = [pltpu.make_async_copy(own_out, dkv_a, st_sem.at[0])]
    stores[0].start()
    for h in range(HEADS):
        cols = pl.ds(h * HD, HD)
        pltpu.make_async_copy(dq.at[pl.ds(h * ALEN, ALEN)], dq_a.at[:, cols], st_sem.at[1]).start()
        pltpu.make_async_copy(dq.at[pl.ds(A_ROWS + h * PIECE, PIECE)], dq_p.at[:, cols], st_sem.at[1]).start()
    while knext >= 1:
        ring(K, knext)
        knext -= 1
    finish(K)
    settle(V)
    settle(K)
    out = pltpu.make_async_copy(prm_out, dkv_p, st_sem.at[2])
    out.start()
    stores[0].wait()
    pltpu.make_async_copy(dq, dq, st_sem.at[1]).wait()
    out.wait()


def per_device(nz, q_ans, kv_ans, q_prompt, kv_prompt, dout_ans, dout_prompt, ans_len, prompt_len):
    half = nz // 2
    n_keys = 256 * half + 128
    any_spec = pl.BlockSpec(memory_space=pl.ANY)
    smem = pl.BlockSpec(memory_space=pltpu.SMEM)
    dma, vm = pltpu.SemaphoreType.DMA, pltpu.VMEM
    blocks = (half, 2, 2, 2)
    return pl.pallas_call(
        functools.partial(kernel, nz),
        out_shape=(
            jax.ShapeDtypeStruct(q_ans.shape, BF16),
            jax.ShapeDtypeStruct(kv_ans.shape, BF16),
            jax.ShapeDtypeStruct(q_prompt.shape, BF16),
            jax.ShapeDtypeStruct(kv_prompt.shape, BF16),
        ),
        in_specs=[smem, smem] + [any_spec] * 6,
        out_specs=(any_spec,) * 4,
        scratch_shapes=[
            vm((n_keys // PIECE, 2, PIECE, HD), BF16),
            vm((HD, n_keys), BF16),
            vm((ROWS, HD), BF16),
            vm((ROWS, HD), BF16),
            vm((n_keys, ROWS), F32),
            vm((n_keys, ROWS), F32),
            vm((n_keys, ROWS), BF16),
            vm((256, ROWS), BF16),
            vm((8, ROWS), F32),
            vm((8, ROWS), F32),
            vm((half + 1, 8, ROWS), F32),
            vm((half + 1, 8, ROWS), F32),
            vm((8, ROWS), F32),
            vm((2, n_keys, HD), F32),
            vm((ROWS, HD), BF16),
            vm((2, ALEN, HD), BF16),
            vm((2, PIECE, HD), BF16),
            vm(blocks + (PIECE, HD), BF16),
            vm(blocks + (PIECE, HD), BF16),
            vm((2, PIECE, HD), BF16),
            vm((2, PIECE, HD), BF16),
            dma((5,)), dma((3,)),
            dma((2, 2)), dma((half, 2, 2)), dma(()), dma(()),
            dma((2, 2)), dma((half, 2, 2)), dma((2,)), dma((2,)),
        ],
        compiler_params=pltpu.CompilerParams(
            collective_id=0, has_side_effects=True, vmem_limit_bytes=58 * 1024 * 1024),
    )(ans_len, prompt_len, q_ans, kv_ans, q_prompt, kv_prompt, dout_ans, dout_prompt)


def solution(mesh):
    in_specs = (
        P(("group", "ans"), "tp"),
        P(None, ("group", "ans"), "tp"),
        P(("group", "ans"), "tp"),
        P(None, ("group", "ans"), "tp"),
        P(("group", "ans"), "tp"),
        P(("group", "ans"), "tp"),
        P(("group", "ans")),
        P("group"),
    )
    out_specs = (
        P(("group", "ans"), "tp"),
        P(None, ("group", "ans"), "tp"),
        P(("group", "ans"), "tp"),
        P(None, ("group", "ans"), "tp"),
    )
    return jax.shard_map(
        functools.partial(per_device, mesh.shape["ans"] // 2), mesh=mesh,
        in_specs=in_specs, out_specs=out_specs, check_vma=False)
```

```python
import functools
import math

import jax
import jax.numpy as jnp
from jax import lax
from jax.experimental import pallas as pl
from jax.experimental.pallas import tpu as pltpu
from jax.sharding import PartitionSpec as P

MESH = pl.DeviceIdType.MESH
F32, BF16 = jnp.float32, jnp.bfloat16
HD = 128
HEADS = 8
ALEN = 128
PIECE = 64
A_ROWS = HEADS * ALEN
P_ROWS = HEADS * PIECE
ROWS = A_ROWS + P_ROWS
LANES = 256
CHUNKS = ROWS // LANES
SCALE = 1.0 / math.sqrt(HD)
COEF = SCALE * math.log2(math.e)
NEG = -1e30
NT = (((1,), (1,)), ((), ()))


NEAR = (0, 1, -1, 2)


def kernel(nz, ans_len, prompt_len, q_a, kv_a, q_p, kv_p, g_a, g_p,
           dq_a, dkv_a, dq_p, dkv_p,
           kv, kt, q, g, e, dp, ds, pbuf, mrun, tot, mgrp, rgrp, delta,
           terms, dq, own_out, prm_out,
           x_out, x_in, near_out, near_in, far_out, far_in,
           ld_sem, st_sem, gf_send, gf_recv, gn_send, gn_recv, gx_send, gx_recv,
           sf_send, sf_recv, sn_send, sn_recv, sx_send, sx_recv):
    fars = nz // 4
    last = 2 * fars
    n_keys = 256 * last + 128
    alen = ans_len[0]
    plen = prompt_len[0]
    me = lax.axis_index("ans")
    side = 1 - 2 * (lax.axis_index("group") % 2)
    par = me // nz
    z = me % nz
    cross = {"ans": (1 - par) * nz + z}

    def along(step):
        return (z + side * step + 2 * nz) % nz

    def peer(step):
        return {"ans": par * nz + along(step)}

    barrier = pltpu.get_barrier_semaphore()
    steps = sorted({n % nz for n in (1, -1, 2, -2)} | {4 * f for f in range(1, fars)})
    for other in [peer(step) for step in steps] + [cross]:
        pl.semaphore_signal(barrier, inc=1, device_id=other, device_id_type=MESH)

    loads = [pltpu.make_async_copy(kv_p, kv.at[0], ld_sem.at[2])]
    for i in range(2):
        rows = pl.ds(i * PIECE, PIECE)
        loads.append(pltpu.make_async_copy(kv_a.at[:, rows], kv.at[4 * last + i], ld_sem.at[3 + i]))
    for load in loads:
        load.start()
    for h in range(HEADS):
        cols = pl.ds(h * HD, HD)
        pltpu.make_async_copy(q_a.at[:, cols], q.at[pl.ds(h * ALEN, ALEN)], ld_sem.at[0]).start()
        pltpu.make_async_copy(q_p.at[:, cols], q.at[pl.ds(A_ROWS + h * PIECE, PIECE)], ld_sem.at[0]).start()
        pltpu.make_async_copy(g_a.at[:, cols], g.at[pl.ds(h * ALEN, ALEN)], ld_sem.at[1]).start()
        pltpu.make_async_copy(g_p.at[:, cols], g.at[pl.ds(A_ROWS + h * PIECE, PIECE)], ld_sem.at[1]).start()

    pl.semaphore_wait(barrier, len(steps) + 1)

    def remote(src, dst, send, recv, device):
        return pltpu.make_async_remote_copy(
            src_ref=src, dst_ref=dst, send_sem=send, recv_sem=recv,
            device_id=device, device_id_type=MESH)

    def to_far(f):
        return remote(kv_p, kv.at[8 * f], gf_send.at[f], gf_recv.at[f], peer(4 * f))

    def to_near(f, n, src=None):
        return remote(kv.at[8 * f] if src is None else src, kv.at[8 * f + n],
                      gn_send.at[f, n], gn_recv.at[f, n], peer(NEAR[n]))

    def to_cross(f, n, src=None):
        return remote(kv.at[8 * f + n] if src is None else src, kv.at[8 * f + 4 + n],
                      gx_send.at[f, n], gx_recv.at[f, n], cross)

    for f in range(1, fars):
        to_far(f).start()
    for n in range(1, 4):
        to_near(0, n, kv_p).start()
    to_cross(0, 0, kv_p).start()

    pltpu.make_async_copy(q, q, ld_sem.at[0]).wait()
    pltpu.make_async_copy(g, g, ld_sem.at[1]).wait()
    for load in loads:
        load.wait()
    tok = lax.broadcasted_iota(jnp.int32, (A_ROWS, HD), 0) & (ALEN - 1)
    g[0:A_ROWS] = jnp.where(tok < alen, g[0:A_ROWS], jnp.zeros((), BF16))
    tok = me * PIECE + (lax.broadcasted_iota(jnp.int32, (P_ROWS, HD), 0) & (PIECE - 1))
    g[A_ROWS:ROWS] = jnp.where(tok < plen, g[A_ROWS:ROWS], jnp.zeros((), BF16))

    def rows_of(s):
        return pl.multiple_of(s * 256, 256) if not isinstance(s, int) else s * 256

    def limits(j):
        lane = lax.broadcasted_iota(jnp.int32, (1, LANES), 1)
        if j * LANES < A_ROWS:
            return jnp.zeros((1, LANES), jnp.int32) + (plen - 1), lane & (ALEN - 1)
        pos = me * PIECE + (lane & (PIECE - 1))
        return jnp.minimum(pos, plen - 1), jnp.full((1, LANES), -1, jnp.int32)

    def score_group(s, bases, own=False):
        n = PIECE * len(bases) + (ALEN if own else 0)
        rows = pl.ds(rows_of(s), n)
        slots = pl.ds(4 * s, n // PIECE)
        keys = kv[slots, 0].reshape(n, HD)
        values = kv[slots, 1].reshape(n, HD)
        for j in range(CHUNKS):
            lanes = slice(j * LANES, (j + 1) * LANES)
            lim, lim_own = limits(j)
            raw = lax.dot_general(keys, q[lanes, :], NT, preferred_element_type=F32)
            parts = []
            for b, base in enumerate(bases):
                pos = base + lax.broadcasted_iota(jnp.int32, (PIECE, LANES), 0)
                parts.append(jnp.where(pos <= lim, raw[b * PIECE:(b + 1) * PIECE], NEG))
            if own:
                pos = lax.broadcasted_iota(jnp.int32, (ALEN, LANES), 0)
                parts.append(jnp.where(pos <= lim_own, raw[n - ALEN:n], NEG))
            raw = jnp.concatenate(parts, 0).reshape(n // 8, 8, LANES)
            high = jnp.max(raw, axis=0)
            if own:
                new = high
            else:
                old = mrun[:, lanes]
                new = jnp.maximum(old, high)
            ex = jnp.exp2((raw - new[None]) * COEF)
            part = jnp.sum(ex, axis=0)
            if own:
                tot[:, lanes] = part
            else:
                tot[:, lanes] = tot[:, lanes] * jnp.exp2((old - new) * COEF) + part
            mrun[:, lanes] = new
            mgrp[s, :, lanes] = new
            e[rows, lanes] = ex.reshape(n, LANES)
            dp[rows, lanes] = lax.dot_general(values, g[lanes, :], NT, preferred_element_type=F32)

    def bases(f, k):
        half = par if k == 0 else 1 - par
        return [(half * nz + along(-(NEAR[n] + 4 * f))) * PIECE for n in range(4)]

    score_group(last, [], True)
    for f in range(1, fars):
        to_far(f).wait_recv()
        for n in range(1, 4):
            to_near(f, n).start()
        to_cross(f, 0).start()

    def this_half(f, carry):
        for n in range(1, 4):
            to_near(f, n).wait_recv()
            to_cross(f, n).start()
        score_group(2 * f, bases(f, 0))
        return carry

    def other_half(f, carry):
        for n in range(4):
            to_cross(f, n).wait_recv()
        score_group(2 * f + 1, bases(f, 1))
        return carry

    lax.fori_loop(0, fars, this_half, 0)
    lax.fori_loop(0, fars, other_half, 0)

    m8 = mrun[...]
    top = jnp.max(m8, axis=0, keepdims=True)
    total = jnp.sum(tot[...] * jnp.exp2((m8 - top) * COEF), axis=0, keepdims=True)
    inv = 1.0 / total
    for s in range(last + 1):
        rgrp[s] = jnp.exp2((mgrp[s] - top) * COEF) * inv
    delta[...] = jnp.zeros_like(delta)

    def value_terms(s, n=256):
        rows = pl.ds(rows_of(s), n)
        for j in range(CHUNKS):
            lanes = slice(j * LANES, (j + 1) * LANES)
            p = e[rows, lanes].reshape(n // 8, 8, LANES) * rgrp[s, :, lanes][None]
            pb = p.reshape(n, LANES).astype(BF16)
            pbuf[0:n, lanes] = pb
            prod = pb.astype(F32) * dp[rows, lanes]
            delta[:, lanes] += jnp.sum(prod.reshape(n // 8, 8, LANES), axis=0)
        terms[1, rows, :] = jnp.dot(pbuf[0:n], g[...], preferred_element_type=F32)

    def key_terms(s, n=256):
        rows = pl.ds(rows_of(s), n)
        for j in range(CHUNKS):
            lanes = slice(j * LANES, (j + 1) * LANES)
            p = e[rows, lanes].reshape(n // 8, 8, LANES) * (rgrp[s, :, lanes] * SCALE)[None]
            diff = dp[rows, lanes].reshape(n // 8, 8, LANES) - delta[:, lanes][None]
            ds[rows, lanes] = (p * diff).reshape(n, LANES).astype(BF16)
        terms[0, rows, :] = jnp.dot(ds[rows, :], q[...], preferred_element_type=F32)

    def query_terms(j):
        lanes = slice(j * LANES, (j + 1) * LANES)
        flipped = jnp.dot(kt[...], ds[:, lanes], preferred_element_type=F32)
        dq[lanes, :] = flipped.T.astype(BF16)

    def sum_cross(c, f):
        return remote(x_out.at[c, f], x_in.at[c, f], sx_send.at[c, f], sx_recv.at[c, f], cross)

    def sum_near(c, f, n):
        return remote(near_out.at[c, f, n - 1], near_in.at[c, f, n - 1],
                      sn_send.at[c, f, n - 1], sn_recv.at[c, f, n - 1], peer(-NEAR[n]))

    def sum_far(c, f):
        return remote(far_out.at[c, f - 1], far_in.at[c, f - 1],
                      sf_send.at[c, f - 1], sf_recv.at[c, f - 1], peer(-4 * f))

    def send_cross(c, f):
        x_out[c, f] = terms[c, pl.ds(rows_of(2 * f + 1), 256), :].astype(BF16)
        sum_cross(c, f).start()

    def send_near(c, f):
        sum_cross(c, f).wait_recv()
        row = 512 * f
        for n in range(1, 4):
            part = terms[c, row + n * PIECE:row + (n + 1) * PIECE, :]
            part = part + x_in[c, f, n * PIECE:(n + 1) * PIECE, :].astype(F32)
            near_out[c, f, n - 1] = part.astype(BF16)
            sum_near(c, f, n).start()

    def held(c, f):
        row = 512 * f
        acc = terms[c, row:row + PIECE, :] + x_in[c, f, 0:PIECE, :].astype(F32)
        for n in range(1, 4):
            sum_near(c, f, n).wait_recv()
            acc = acc + near_in[c, f, n - 1].astype(F32)
        return acc

    def send_far(c, f):
        far_out[c, f - 1] = held(c, f).astype(BF16)
        sum_far(c, f).start()

    def finish(c):
        acc = held(c, 0)
        for f in range(1, fars):
            sum_far(c, f).wait_recv()
            acc = acc + far_in[c, f - 1].astype(F32)
        prm_out[c] = acc.astype(BF16)

    K, V = 0, 1

    def value_cross(i, carry):
        f = fars - 1 - i
        value_terms(2 * f + 1)
        send_cross(V, f)
        return carry

    def key_cross(i, carry):
        f = fars - 1 - i
        key_terms(2 * f + 1)
        send_cross(K, f)
        return carry

    lax.fori_loop(0, fars, value_cross, 0)
    value_terms(last, 128)
    lax.fori_loop(0, fars, lambda i, carry: (value_terms(2 * (fars - 1 - i)), carry)[1], 0)
    delta[...] = jnp.broadcast_to(jnp.sum(delta[...], axis=0, keepdims=True), delta.shape)
    lax.fori_loop(0, fars, key_cross, 0)
    for f in range(fars - 1, fars // 2 - 1, -1):
        send_near(V, f)
    lax.fori_loop(0, fars // 2, lambda i, carry: (key_terms(2 * (fars - 1 - i)), carry)[1], 0)
    for f in range(fars // 2 - 1, -1, -1):
        send_near(V, f)
    lax.fori_loop(fars // 2, fars, lambda i, carry: (key_terms(2 * (fars - 1 - i)), carry)[1], 0)
    key_terms(last, 128)
    own_out[...] = terms[:, 256 * last:256 * last + ALEN, :].astype(BF16)
    own_store = pltpu.make_async_copy(own_out, dkv_a, st_sem.at[0])
    own_store.start()
    for s in range(n_keys // 128):
        kt[:, s * 128:(s + 1) * 128] = kv[2 * s:2 * s + 2, 0].reshape(128, HD).T
    query_terms(0)
    query_terms(1)
    todo_near = list(range(fars - 1, -1, -1))
    todo_far = list(range(fars - 1, 0, -1))
    for f in todo_far:
        send_far(V, f)
    send_near(K, todo_near.pop(0))
    query_terms(2)
    query_terms(3)
    send_near(K, todo_near.pop(0))
    query_terms(4)
    query_terms(5)
    for h in range(HEADS):
        cols = pl.ds(h * HD, HD)
        pltpu.make_async_copy(dq.at[pl.ds(h * ALEN, ALEN)], dq_a.at[:, cols], st_sem.at[1]).start()
        pltpu.make_async_copy(dq.at[pl.ds(A_ROWS + h * PIECE, PIECE)], dq_p.at[:, cols], st_sem.at[1]).start()
    for f in todo_near:
        send_near(K, f)
    for f in todo_far:
        send_far(K, f)
    finish(V)
    finish(K)
    out = pltpu.make_async_copy(prm_out, dkv_p, st_sem.at[2])
    out.start()

    for f in range(fars):
        for n in range(4):
            to_cross(f, n).wait_send()
            if n:
                to_near(f, n).wait_send()
        if f:
            to_far(f).wait_send()
        for c in range(2):
            sum_cross(c, f).wait_send()
            for n in range(1, 4):
                sum_near(c, f, n).wait_send()
            if f:
                sum_far(c, f).wait_send()
    own_store.wait()
    pltpu.make_async_copy(dq, dq, st_sem.at[1]).wait()
    out.wait()


def deliver(*refs):
    sems = refs[-1]
    count = len(refs) // 2
    copies = [pltpu.make_async_copy(refs[i], refs[count + i], sems.at[i]) for i in range(count)]
    for copy in copies:
        copy.start()
    for copy in copies:
        copy.wait()


def per_device(nz, q_ans, kv_ans, q_prompt, kv_prompt, dout_ans, dout_prompt, ans_len, prompt_len):
    fars = nz // 4
    groups = 2 * fars + 1
    n_keys = 512 * fars + 128
    any_spec = pl.BlockSpec(memory_space=pl.ANY)
    smem = pl.BlockSpec(memory_space=pltpu.SMEM)
    dma, vm = pltpu.SemaphoreType.DMA, pltpu.VMEM
    out_shape = tuple(jax.ShapeDtypeStruct(a.shape, BF16) for a in (q_ans, kv_ans, q_prompt, kv_prompt))
    results = pl.pallas_call(
        functools.partial(kernel, nz),
        out_shape=out_shape,
        in_specs=[smem, smem] + [any_spec] * 6,
        out_specs=(any_spec,) * 4,
        scratch_shapes=[
            vm((n_keys // PIECE, 2, PIECE, HD), BF16),
            vm((HD, n_keys), BF16),
            vm((ROWS, HD), BF16),
            vm((ROWS, HD), BF16),
            vm((n_keys, ROWS), F32),
            vm((n_keys, ROWS), F32),
            vm((n_keys, ROWS), BF16),
            vm((256, ROWS), BF16),
            vm((8, ROWS), F32),
            vm((8, ROWS), F32),
            vm((groups, 8, ROWS), F32),
            vm((groups, 8, ROWS), F32),
            vm((8, ROWS), F32),
            vm((2, n_keys, HD), F32),
            vm((ROWS, HD), BF16),
            vm((2, ALEN, HD), BF16),
            vm((2, PIECE, HD), BF16),
            vm((2, fars, 256, HD), BF16), vm((2, fars, 256, HD), BF16),
            vm((2, fars, 3, PIECE, HD), BF16), vm((2, fars, 3, PIECE, HD), BF16),
            vm((2, fars - 1, PIECE, HD), BF16), vm((2, fars - 1, PIECE, HD), BF16),
            dma((5,)), dma((3,)),
            dma((fars,)), dma((fars,)), dma((fars, 4)), dma((fars, 4)), dma((fars, 4)), dma((fars, 4)),
            dma((2, fars - 1)), dma((2, fars - 1)), dma((2, fars, 3)), dma((2, fars, 3)),
            dma((2, fars)), dma((2, fars)),
        ],
        compiler_params=pltpu.CompilerParams(
            collective_id=0, has_side_effects=True, vmem_limit_bytes=58 * 1024 * 1024),
    )(ans_len, prompt_len, q_ans, kv_ans, q_prompt, kv_prompt, dout_ans, dout_prompt)
    return pl.pallas_call(
        deliver, out_shape=out_shape, in_specs=[any_spec] * 4, out_specs=(any_spec,) * 4,
        scratch_shapes=[dma((4,))],
    )(*results)


def solution(mesh):
    in_specs = (
        P(("group", "ans"), "tp"),
        P(None, ("group", "ans"), "tp"),
        P(("group", "ans"), "tp"),
        P(None, ("group", "ans"), "tp"),
        P(("group", "ans"), "tp"),
        P(("group", "ans"), "tp"),
        P(("group", "ans")),
        P("group"),
    )
    out_specs = (
        P(("group", "ans"), "tp"),
        P(None, ("group", "ans"), "tp"),
        P(("group", "ans"), "tp"),
        P(None, ("group", "ans"), "tp"),
    )
    return jax.shard_map(
        functools.partial(per_device, mesh.shape["ans"] // 2), mesh=mesh,
        in_specs=in_specs, out_specs=out_specs, check_vma=False)
```

```python
import functools
import math

import jax
import jax.numpy as jnp
from jax import lax
from jax.experimental import pallas as pl
from jax.experimental.pallas import tpu as pltpu
from jax.sharding import PartitionSpec as P

MESH = pl.DeviceIdType.MESH
F32, BF16 = jnp.float32, jnp.bfloat16
HD = 128
HEADS = 8
ALEN = 128
PIECE = 64
A_ROWS = HEADS * ALEN
P_ROWS = HEADS * PIECE
ROWS = A_ROWS + P_ROWS
LANES = 256
CHUNKS = ROWS // LANES
SCALE = 1.0 / math.sqrt(HD)
COEF = SCALE * math.log2(math.e)
NEG = -1e30
NT = (((1,), (1,)), ((), ()))


NEAR = (0, 1, -1, 2)


def kernel(nz, ans_len, prompt_len, q_a, kv_a, q_p, kv_p, g_a, g_p,
           dq_a, dkv_a, dq_p, dkv_p,
           kv, kt, q, g, e, dp, ds, mrun, tot, mgrp, rgrp, delta, terms,
           x_out, x_in, near_out, near_in, far_out, far_in,
           ld_sem, gf_send, gf_recv, gn_send, gn_recv, gx_send, gx_recv,
           sf_send, sf_recv, sn_send, sn_recv, sx_send, sx_recv):
    fars = nz // 4
    last = 2 * fars
    n_keys = 256 * last + 128
    alen = ans_len[0]
    plen = prompt_len[0]
    me = lax.axis_index("ans")
    side = 1 - 2 * (lax.axis_index("group") % 2)
    par = me // nz
    z = me % nz
    cross = {"ans": (1 - par) * nz + z}

    def along(step):
        return (z + side * step + 2 * nz) % nz

    def peer(step):
        return {"ans": par * nz + along(step)}

    barrier = pltpu.get_barrier_semaphore()
    steps = sorted({n % nz for n in (1, -1, 2, -2)} | {4 * f for f in range(1, fars)})
    for other in [peer(step) for step in steps] + [cross]:
        pl.semaphore_signal(barrier, inc=1, device_id=other, device_id_type=MESH)

    loads = [pltpu.make_async_copy(kv_p, kv.at[0], ld_sem.at[2])]
    for i in range(2):
        rows = pl.ds(i * PIECE, PIECE)
        loads.append(pltpu.make_async_copy(kv_a.at[:, rows], kv.at[4 * last + i], ld_sem.at[3 + i]))
    for load in loads:
        load.start()
    for h in range(HEADS):
        cols = pl.ds(h * HD, HD)
        pltpu.make_async_copy(q_a.at[:, cols], q.at[pl.ds(h * ALEN, ALEN)], ld_sem.at[0]).start()
        pltpu.make_async_copy(q_p.at[:, cols], q.at[pl.ds(A_ROWS + h * PIECE, PIECE)], ld_sem.at[0]).start()
        pltpu.make_async_copy(g_a.at[:, cols], g.at[pl.ds(h * ALEN, ALEN)], ld_sem.at[1]).start()
        pltpu.make_async_copy(g_p.at[:, cols], g.at[pl.ds(A_ROWS + h * PIECE, PIECE)], ld_sem.at[1]).start()

    pl.semaphore_wait(barrier, len(steps) + 1)

    def remote(src, dst, send, recv, device):
        return pltpu.make_async_remote_copy(
            src_ref=src, dst_ref=dst, send_sem=send, recv_sem=recv,
            device_id=device, device_id_type=MESH)

    def to_far(c, f):
        return remote(kv_p.at[c], kv.at[8 * f, c], gf_send.at[c, f], gf_recv.at[c, f], peer(4 * f))

    def to_near(c, f, n, src=None):
        return remote(kv.at[8 * f, c] if src is None else src, kv.at[8 * f + n, c],
                      gn_send.at[c, f, n], gn_recv.at[c, f, n], peer(NEAR[n]))

    def to_cross(c, f, n, src=None):
        return remote(kv.at[8 * f + n, c] if src is None else src, kv.at[8 * f + 4 + n, c],
                      gx_send.at[c, f, n], gx_recv.at[c, f, n], cross)

    def spread_own(c):
        for n in range(1, 4):
            to_near(c, 0, n, kv_p.at[c]).start()
        to_cross(c, 0, 0, kv_p.at[c]).start()

    def spread_far(c):
        for f in range(1, fars):
            to_far(c, f).wait_recv()
            for n in range(1, 4):
                to_near(c, f, n).start()
            to_cross(c, f, 0).start()

    K, V = 0, 1
    for f in range(1, fars):
        to_far(K, f).start()
    spread_own(K)
    for f in range(1, fars):
        to_far(V, f).start()

    pltpu.make_async_copy(q, q, ld_sem.at[0]).wait()
    pltpu.make_async_copy(g, g, ld_sem.at[1]).wait()
    for load in loads:
        load.wait()
    tok = lax.broadcasted_iota(jnp.int32, (A_ROWS, HD), 0) & (ALEN - 1)
    g[0:A_ROWS] = jnp.where(tok < alen, g[0:A_ROWS], jnp.zeros((), BF16))
    tok = me * PIECE + (lax.broadcasted_iota(jnp.int32, (P_ROWS, HD), 0) & (PIECE - 1))
    g[A_ROWS:ROWS] = jnp.where(tok < plen, g[A_ROWS:ROWS], jnp.zeros((), BF16))

    def rows_of(s):
        return pl.multiple_of(s * 256, 256) if not isinstance(s, int) else s * 256

    def limits(j):
        lane = lax.broadcasted_iota(jnp.int32, (1, LANES), 1)
        if j * LANES < A_ROWS:
            return jnp.zeros((1, LANES), jnp.int32) + (plen - 1), lane & (ALEN - 1)
        pos = me * PIECE + (lane & (PIECE - 1))
        return jnp.minimum(pos, plen - 1), jnp.full((1, LANES), -1, jnp.int32)

    def score_group(s, bases, own=False):
        n = PIECE * len(bases) + (ALEN if own else 0)
        rows = pl.ds(rows_of(s), n)
        slots = pl.ds(4 * s, n // PIECE)
        keys = kv[slots, 0].reshape(n, HD)
        for j in range(CHUNKS):
            lanes = slice(j * LANES, (j + 1) * LANES)
            lim, lim_own = limits(j)
            raw = lax.dot_general(keys, q[lanes, :], NT, preferred_element_type=F32)
            parts = []
            for b, base in enumerate(bases):
                pos = base + lax.broadcasted_iota(jnp.int32, (PIECE, LANES), 0)
                parts.append(jnp.where(pos <= lim, raw[b * PIECE:(b + 1) * PIECE], NEG))
            if own:
                pos = lax.broadcasted_iota(jnp.int32, (ALEN, LANES), 0)
                parts.append(jnp.where(pos <= lim_own, raw[n - ALEN:n], NEG))
            raw = jnp.concatenate(parts, 0).reshape(n // 8, 8, LANES)
            high = jnp.max(raw, axis=0)
            if own:
                new = high
            else:
                old = mrun[:, lanes]
                new = jnp.maximum(old, high)
            ex = jnp.exp2((raw - new[None]) * COEF)
            part = jnp.sum(ex, axis=0)
            if own:
                tot[:, lanes] = part
            else:
                tot[:, lanes] = tot[:, lanes] * jnp.exp2((old - new) * COEF) + part
            mrun[:, lanes] = new
            mgrp[s, :, lanes] = new
            e[rows, lanes] = ex.reshape(n, LANES)

    def bases(f, k):
        half = par if k == 0 else 1 - par
        return [(half * nz + along(-(NEAR[n] + 4 * f))) * PIECE for n in range(4)]

    score_group(last, [], True)
    spread_far(K)

    def this_half(f, carry):
        for n in range(1, 4):
            to_near(K, f, n).wait_recv()
            to_cross(K, f, n).start()
        score_group(2 * f, bases(f, 0))
        return carry

    def other_half(f, carry):
        for n in range(4):
            to_cross(K, f, n).wait_recv()
        score_group(2 * f + 1, bases(f, 1))
        return carry

    lax.fori_loop(0, fars, this_half, 0)
    spread_own(V)
    spread_far(V)
    lax.fori_loop(0, fars, other_half, 0)

    def values_on(f, carry):
        for n in range(1, 4):
            to_near(V, f, n).wait_recv()
            to_cross(V, f, n).start()
        return carry

    lax.fori_loop(0, fars, values_on, 0)

    m8 = mrun[...]
    top = jnp.max(m8, axis=0, keepdims=True)
    total = jnp.sum(tot[...] * jnp.exp2((m8 - top) * COEF), axis=0, keepdims=True)
    inv = 1.0 / total
    for s in range(last + 1):
        rgrp[s] = jnp.exp2((mgrp[s] - top) * COEF) * inv
    delta[...] = jnp.zeros_like(delta)

    def value_terms(s, n=256):
        rows = pl.ds(rows_of(s), n)
        for j in range(CHUNKS):
            lanes = slice(j * LANES, (j + 1) * LANES)
            p = e[rows, lanes].reshape(n // 8, 8, LANES) * rgrp[s, :, lanes][None]
            ds[rows, lanes] = p.reshape(n, LANES).astype(BF16)
        terms[1, rows, :] = jnp.dot(ds[rows, :], g[...], preferred_element_type=F32)

    def delta_terms(s, n=256):
        rows = pl.ds(rows_of(s), n)
        values = kv[pl.ds(4 * s, n // PIECE), 1].reshape(n, HD)
        for j in range(CHUNKS):
            lanes = slice(j * LANES, (j + 1) * LANES)
            dprob = lax.dot_general(values, g[lanes, :], NT, preferred_element_type=F32)
            dp[rows, lanes] = dprob
            prod = ds[rows, lanes].astype(F32) * dprob
            delta[:, lanes] += jnp.sum(prod.reshape(n // 8, 8, LANES), axis=0)

    def key_terms(s, n=256):
        rows = pl.ds(rows_of(s), n)
        for j in range(CHUNKS):
            lanes = slice(j * LANES, (j + 1) * LANES)
            p = e[rows, lanes].reshape(n // 8, 8, LANES) * (rgrp[s, :, lanes] * SCALE)[None]
            diff = dp[rows, lanes].reshape(n // 8, 8, LANES) - delta[:, lanes][None]
            ds[rows, lanes] = (p * diff).reshape(n, LANES).astype(BF16)
        terms[0, rows, :] = jnp.dot(ds[rows, :], q[...], preferred_element_type=F32)

    def query_terms(j):
        lanes = slice(j * LANES, (j + 1) * LANES)
        rows = jnp.dot(kt[...], ds[:, lanes], preferred_element_type=F32).T.astype(BF16)
        out, tokens, first = (dq_a, ALEN, j * LANES) if j * LANES < A_ROWS else (dq_p, PIECE, j * LANES - A_ROWS)
        for i in range(LANES // tokens):
            head = first // tokens + i
            out[:, head * HD:(head + 1) * HD] = rows[i * tokens:(i + 1) * tokens]

    def sum_cross(c, f):
        return remote(x_out.at[c, f], x_in.at[c, f], sx_send.at[c, f], sx_recv.at[c, f], cross)

    def sum_near(c, f, n):
        return remote(near_out.at[c, f, n - 1], near_in.at[c, f, n - 1],
                      sn_send.at[c, f, n - 1], sn_recv.at[c, f, n - 1], peer(-NEAR[n]))

    def sum_far(c, f):
        return remote(far_out.at[c, f - 1], far_in.at[c, f - 1],
                      sf_send.at[c, f - 1], sf_recv.at[c, f - 1], peer(-4 * f))

    def send_cross(c, f):
        x_out[c, f] = terms[c, pl.ds(rows_of(2 * f + 1), 256), :].astype(BF16)
        sum_cross(c, f).start()

    def send_near(c, f):
        sum_cross(c, f).wait_recv()
        row = 512 * f
        for n in range(1, 4):
            part = terms[c, row + n * PIECE:row + (n + 1) * PIECE, :]
            part = part + x_in[c, f, n * PIECE:(n + 1) * PIECE, :].astype(F32)
            near_out[c, f, n - 1] = part.astype(BF16)
            sum_near(c, f, n).start()

    def held(c, f):
        row = 512 * f
        acc = terms[c, row:row + PIECE, :] + x_in[c, f, 0:PIECE, :].astype(F32)
        for n in range(1, 4):
            sum_near(c, f, n).wait_recv()
            acc = acc + near_in[c, f, n - 1].astype(F32)
        return acc

    def send_far(c, f):
        far_out[c, f - 1] = held(c, f).astype(BF16)
        sum_far(c, f).start()

    def finish(c):
        acc = held(c, 0)
        for f in range(1, fars):
            sum_far(c, f).wait_recv()
            acc = acc + far_in[c, f - 1].astype(F32)
        dkv_p[c] = acc.astype(BF16)

    def value_cross(i, carry):
        f = fars - 1 - i
        value_terms(2 * f + 1)
        send_cross(V, f)
        return carry

    def key_cross(i, carry):
        f = fars - 1 - i
        key_terms(2 * f + 1)
        send_cross(K, f)
        return carry

    def own_delta(f, carry):
        delta_terms(2 * f)
        return carry

    def cross_delta(f, carry):
        for n in range(4):
            to_cross(V, f, n).wait_recv()
        delta_terms(2 * f + 1)
        return carry

    lax.fori_loop(0, fars, value_cross, 0)
    value_terms(last, 128)
    lax.fori_loop(0, fars, lambda i, carry: (value_terms(2 * (fars - 1 - i)), carry)[1], 0)
    delta_terms(last, 128)
    lax.fori_loop(0, fars, own_delta, 0)
    lax.fori_loop(0, fars, cross_delta, 0)
    delta[...] = jnp.broadcast_to(jnp.sum(delta[...], axis=0, keepdims=True), delta.shape)
    for f in range(fars - 1, fars // 2 - 1, -1):
        send_near(V, f)
    lax.fori_loop(0, fars, key_cross, 0)
    for f in range(fars // 2 - 1, -1, -1):
        send_near(V, f)
    lax.fori_loop(0, fars, lambda i, carry: (key_terms(2 * (fars - 1 - i)), carry)[1], 0)
    key_terms(last, 128)
    dkv_a[...] = terms[:, 256 * last:256 * last + ALEN, :].astype(BF16)
    for s in range(n_keys // 128):
        kt[:, s * 128:(s + 1) * 128] = kv[2 * s:2 * s + 2, 0].reshape(128, HD).T
    query_terms(0)
    query_terms(1)
    todo_near = list(range(fars - 1, -1, -1))
    todo_far = list(range(fars - 1, 0, -1))
    for f in todo_far:
        send_far(V, f)
    send_near(K, todo_near.pop(0))
    query_terms(2)
    query_terms(3)
    send_near(K, todo_near.pop(0))
    query_terms(4)
    query_terms(5)
    for f in todo_near:
        send_near(K, f)
    for f in todo_far:
        send_far(K, f)
    finish(V)
    finish(K)
    for c in range(2):
        for f in range(fars):
            for n in range(4):
                to_cross(c, f, n).wait_send()
                if n:
                    to_near(c, f, n).wait_send()
                    sum_near(c, f, n).wait_send()
            sum_cross(c, f).wait_send()
            if f:
                to_far(c, f).wait_send()
                sum_far(c, f).wait_send()


def deliver(*refs):
    sems = refs[-1]
    count = len(refs) // 2
    copies = [pltpu.make_async_copy(refs[i], refs[count + i], sems.at[i]) for i in range(count)]
    for copy in copies:
        copy.start()
    for copy in copies:
        copy.wait()


def per_device(nz, q_ans, kv_ans, q_prompt, kv_prompt, dout_ans, dout_prompt, ans_len, prompt_len):
    fars = nz // 4
    groups = 2 * fars + 1
    n_keys = 512 * fars + 128
    any_spec = pl.BlockSpec(memory_space=pl.ANY)
    smem = pl.BlockSpec(memory_space=pltpu.SMEM)
    dma, vm = pltpu.SemaphoreType.DMA, pltpu.VMEM
    out_shape = tuple(jax.ShapeDtypeStruct(a.shape, BF16) for a in (q_ans, kv_ans, q_prompt, kv_prompt))
    results = pl.pallas_call(
        functools.partial(kernel, nz),
        out_shape=tuple(vm(a.shape, BF16) for a in (q_ans, kv_ans, q_prompt, kv_prompt)),
        in_specs=[smem, smem] + [any_spec] * 6,
        out_specs=(pl.BlockSpec(memory_space=vm),) * 4,
        scratch_shapes=[
            vm((n_keys // PIECE, 2, PIECE, HD), BF16),
            vm((HD, n_keys), BF16),
            vm((ROWS, HD), BF16),
            vm((ROWS, HD), BF16),
            vm((n_keys, ROWS), F32),
            vm((n_keys, ROWS), F32),
            vm((n_keys, ROWS), BF16),
            vm((8, ROWS), F32),
            vm((8, ROWS), F32),
            vm((groups, 8, ROWS), F32),
            vm((groups, 8, ROWS), F32),
            vm((8, ROWS), F32),
            vm((2, n_keys, HD), F32),
            vm((2, fars, 256, HD), BF16), vm((2, fars, 256, HD), BF16),
            vm((2, fars, 3, PIECE, HD), BF16), vm((2, fars, 3, PIECE, HD), BF16),
            vm((2, fars - 1, PIECE, HD), BF16), vm((2, fars - 1, PIECE, HD), BF16),
            dma((5,)),
            dma((2, fars)), dma((2, fars)), dma((2, fars, 4)), dma((2, fars, 4)), dma((2, fars, 4)), dma((2, fars, 4)),
            dma((2, fars - 1)), dma((2, fars - 1)), dma((2, fars, 3)), dma((2, fars, 3)),
            dma((2, fars)), dma((2, fars)),
        ],
        compiler_params=pltpu.CompilerParams(
            collective_id=0, has_side_effects=True, vmem_limit_bytes=58 * 1024 * 1024),
    )(ans_len, prompt_len, q_ans, kv_ans, q_prompt, kv_prompt, dout_ans, dout_prompt)
    vm_spec = pl.BlockSpec(memory_space=vm)
    return pl.pallas_call(
        deliver, out_shape=out_shape, in_specs=[vm_spec] * 4, out_specs=(any_spec,) * 4,
        scratch_shapes=[dma((4,))],
    )(*results)


def solution(mesh):
    in_specs = (
        P(("group", "ans"), "tp"),
        P(None, ("group", "ans"), "tp"),
        P(("group", "ans"), "tp"),
        P(None, ("group", "ans"), "tp"),
        P(("group", "ans"), "tp"),
        P(("group", "ans"), "tp"),
        P(("group", "ans")),
        P("group"),
    )
    out_specs = (
        P(("group", "ans"), "tp"),
        P(None, ("group", "ans"), "tp"),
        P(("group", "ans"), "tp"),
        P(None, ("group", "ans"), "tp"),
    )
    return jax.shard_map(
        functools.partial(per_device, mesh.shape["ans"] // 2), mesh=mesh,
        in_specs=in_specs, out_specs=out_specs, check_vma=False)
```

```python
import functools
import math

import jax
import jax.numpy as jnp
from jax import lax
from jax.experimental import pallas as pl
from jax.experimental.pallas import tpu as pltpu
from jax.sharding import PartitionSpec as P

MESH = pl.DeviceIdType.MESH
F32, BF16 = jnp.float32, jnp.bfloat16
HD = 128
HEADS = 8
ALEN = 128
PIECE = 64
A_ROWS = HEADS * ALEN
P_ROWS = HEADS * PIECE
ROWS = A_ROWS + P_ROWS
LANES = 256
CHUNKS = ROWS // LANES
SCALE = 1.0 / math.sqrt(HD)
COEF = SCALE * math.log2(math.e)
NEG = -1e30
NT = (((1,), (1,)), ((), ()))


def far_step(f):
    return 4 * f + f % 2


def near_step(f, n):
    return (0, 1, -1, 2 - 4 * (f % 2))[n]


def kernel(nz, ans_len, prompt_len, q_a, kv_a, q_p, kv_p, g_a, g_p,
           dq_a, dkv_a, dq_p, dkv_p,
           kv, kt, q, g, e, dp, ds, mrun, tot, mgrp, rgrp, delta, terms,
           dq, own_out, prm_out,
           x_out, x_in, near_out, near_in, far_out, far_in,
           ld_sem, st_sem, gf_send, gf_recv, gn_send, gn_recv, gx_send, gx_recv,
           sf_send, sf_recv, sn_send, sn_recv, sx_send, sx_recv):
    fars = nz // 4
    last = 2 * fars
    early = fars // 2
    n_keys = 256 * last + 128
    alen = ans_len[0]
    plen = prompt_len[0]
    me = lax.axis_index("ans")
    side = 1 - 2 * (lax.axis_index("group") % 2)
    par = me // nz
    z = me % nz
    cross = {"ans": (1 - par) * nz + z}

    def along(step):
        return (z + side * step + 4 * nz) % nz

    def peer(step):
        return {"ans": par * nz + along(step)}

    barrier = pltpu.get_barrier_semaphore()
    steps = {n % nz for n in (1, -1, 2, -2)}
    for f in range(1, fars):
        steps |= {far_step(f) % nz, -far_step(f) % nz}
    steps = sorted(steps)
    for other in [peer(step) for step in steps] + [cross]:
        pl.semaphore_signal(barrier, inc=1, device_id=other, device_id_type=MESH)

    loads = [pltpu.make_async_copy(kv_p, kv.at[0], ld_sem.at[2])]
    for i in range(2):
        rows = pl.ds(i * PIECE, PIECE)
        loads.append(pltpu.make_async_copy(kv_a.at[:, rows], kv.at[4 * last + i], ld_sem.at[3 + i]))
    for load in loads:
        load.start()
    for h in range(HEADS):
        cols = pl.ds(h * HD, HD)
        pltpu.make_async_copy(q_a.at[:, cols], q.at[pl.ds(h * ALEN, ALEN)], ld_sem.at[0]).start()
        pltpu.make_async_copy(q_p.at[:, cols], q.at[pl.ds(A_ROWS + h * PIECE, PIECE)], ld_sem.at[0]).start()
        pltpu.make_async_copy(g_a.at[:, cols], g.at[pl.ds(h * ALEN, ALEN)], ld_sem.at[1]).start()
        pltpu.make_async_copy(g_p.at[:, cols], g.at[pl.ds(A_ROWS + h * PIECE, PIECE)], ld_sem.at[1]).start()

    pl.semaphore_wait(barrier, len(steps) + 1)

    def remote(src, dst, send, recv, device):
        return pltpu.make_async_remote_copy(
            src_ref=src, dst_ref=dst, send_sem=send, recv_sem=recv,
            device_id=device, device_id_type=MESH)

    def to_far(c, f):
        return remote(kv_p.at[c], kv.at[8 * f, c], gf_send.at[c, f], gf_recv.at[c, f], peer(far_step(f)))

    def to_near(c, f, k, n, src=None):
        return remote(kv.at[8 * f + 4 * k, c] if src is None else src, kv.at[8 * f + 4 * k + n, c],
                      gn_send.at[c, f, k, n], gn_recv.at[c, f, k, n], peer(near_step(f, n)))

    def to_cross(c, f, n, src=None):
        return remote(kv.at[8 * f + n, c] if src is None else src, kv.at[8 * f + 4 + n, c],
                      gx_send.at[c, f, n], gx_recv.at[c, f, n], cross)

    def spread_own(c):
        to_cross(c, 0, 0, kv_p.at[c]).start()
        for n in range(1, 4):
            to_near(c, 0, 0, n, kv_p.at[c]).start()

    def spread_far(c):
        for f in range(1, fars):
            to_far(c, f).wait_recv()
            to_cross(c, f, 0).start()
            for n in range(1, 4):
                to_near(c, f, 0, n).start()

    def spread_cross(c):
        for f in range(early):
            to_cross(c, f, 0).wait_recv()
            for n in range(1, 4):
                to_near(c, f, 1, n).start()

    def near_arrived(c, f, k):
        for n in range(1, 4):
            to_near(c, f, k, n).wait_recv()

    def near_to_cross(c, f):
        for n in range(1, 4):
            to_near(c, f, 0, n).wait_recv()
            to_cross(c, f, n).start()

    def cross_arrived(c, f):
        for n in range(4):
            to_cross(c, f, n).wait_recv()

    K, V = 0, 1
    for f in range(1, fars):
        to_far(K, f).start()
    spread_own(K)
    for f in range(1, fars):
        to_far(V, f).start()

    pltpu.make_async_copy(q, q, ld_sem.at[0]).wait()
    pltpu.make_async_copy(g, g, ld_sem.at[1]).wait()
    for load in loads:
        load.wait()
    tok = lax.broadcasted_iota(jnp.int32, (A_ROWS, HD), 0) & (ALEN - 1)
    g[0:A_ROWS] = jnp.where(tok < alen, g[0:A_ROWS], jnp.zeros((), BF16))
    tok = me * PIECE + (lax.broadcasted_iota(jnp.int32, (P_ROWS, HD), 0) & (PIECE - 1))
    g[A_ROWS:ROWS] = jnp.where(tok < plen, g[A_ROWS:ROWS], jnp.zeros((), BF16))

    def rows_of(s):
        return pl.multiple_of(s * 256, 256) if not isinstance(s, int) else s * 256

    def limits(j):
        lane = lax.broadcasted_iota(jnp.int32, (1, LANES), 1)
        if j * LANES < A_ROWS:
            return jnp.zeros((1, LANES), jnp.int32) + (plen - 1), lane & (ALEN - 1)
        pos = me * PIECE + (lane & (PIECE - 1))
        return jnp.minimum(pos, plen - 1), jnp.full((1, LANES), -1, jnp.int32)

    def score_group(s, bases, own=False):
        n = PIECE * len(bases) + (ALEN if own else 0)
        rows = pl.ds(rows_of(s), n)
        slots = pl.ds(4 * s, n // PIECE)
        keys = kv[slots, 0].reshape(n, HD)
        for j in range(CHUNKS):
            lanes = slice(j * LANES, (j + 1) * LANES)
            lim, lim_own = limits(j)
            raw = lax.dot_general(keys, q[lanes, :], NT, preferred_element_type=F32)
            parts = []
            for b, base in enumerate(bases):
                pos = base + lax.broadcasted_iota(jnp.int32, (PIECE, LANES), 0)
                parts.append(jnp.where(pos <= lim, raw[b * PIECE:(b + 1) * PIECE], NEG))
            if own:
                pos = lax.broadcasted_iota(jnp.int32, (ALEN, LANES), 0)
                parts.append(jnp.where(pos <= lim_own, raw[n - ALEN:n], NEG))
            raw = jnp.concatenate(parts, 0).reshape(n // 8, 8, LANES)
            high = jnp.max(raw, axis=0)
            if own:
                new = high
            else:
                old = mrun[:, lanes]
                new = jnp.maximum(old, high)
            ex = jnp.exp2((raw - new[None]) * COEF)
            part = jnp.sum(ex, axis=0)
            if own:
                tot[:, lanes] = part
            else:
                tot[:, lanes] = tot[:, lanes] * jnp.exp2((old - new) * COEF) + part
            mrun[:, lanes] = new
            mgrp[s, :, lanes] = new
            e[rows, lanes] = ex.reshape(n, LANES)

    def bases(f, k):
        half = par if k == 0 else 1 - par
        return [(half * nz + along(-(near_step(f, n) + far_step(f)))) * PIECE for n in range(4)]

    def loop(first, stop, *steps):
        def body(i, carry):
            f = first + i if stop >= first else first - 1 - i
            for step in steps:
                step(f)
            return carry
        lax.fori_loop(0, abs(stop - first), body, 0)

    score_group(last, [], True)
    spread_far(K)
    spread_cross(K)
    loop(0, early, lambda f: near_arrived(K, f, 0), lambda f: score_group(2 * f, bases(f, 0)))
    loop(early, fars, lambda f: near_to_cross(K, f), lambda f: score_group(2 * f, bases(f, 0)))
    spread_own(V)
    spread_far(V)
    spread_cross(V)
    loop(0, early, lambda f: near_arrived(K, f, 1), lambda f: score_group(2 * f + 1, bases(f, 1)))
    loop(early, fars, lambda f: cross_arrived(K, f), lambda f: score_group(2 * f + 1, bases(f, 1)))
    for f in range(early, fars):
        near_to_cross(V, f)

    m8 = mrun[...]
    top = jnp.max(m8, axis=0, keepdims=True)
    total = jnp.sum(tot[...] * jnp.exp2((m8 - top) * COEF), axis=0, keepdims=True)
    inv = 1.0 / total
    for s in range(last + 1):
        rgrp[s] = jnp.exp2((mgrp[s] - top) * COEF) * inv
    delta[...] = jnp.zeros_like(delta)

    def value_terms(s, n=256):
        rows = pl.ds(rows_of(s), n)
        for j in range(CHUNKS):
            lanes = slice(j * LANES, (j + 1) * LANES)
            p = e[rows, lanes].reshape(n // 8, 8, LANES) * rgrp[s, :, lanes][None]
            ds[rows, lanes] = p.reshape(n, LANES).astype(BF16)
        terms[1, rows, :] = jnp.dot(ds[rows, :], g[...], preferred_element_type=F32)

    def delta_terms(s, n=256):
        rows = pl.ds(rows_of(s), n)
        values = kv[pl.ds(4 * s, n // PIECE), 1].reshape(n, HD)
        for j in range(CHUNKS):
            lanes = slice(j * LANES, (j + 1) * LANES)
            dprob = lax.dot_general(values, g[lanes, :], NT, preferred_element_type=F32)
            dp[rows, lanes] = dprob
            prod = ds[rows, lanes].astype(F32) * dprob
            delta[:, lanes] += jnp.sum(prod.reshape(n // 8, 8, LANES), axis=0)

    def key_terms(s, n=256):
        rows = pl.ds(rows_of(s), n)
        for j in range(CHUNKS):
            lanes = slice(j * LANES, (j + 1) * LANES)
            p = e[rows, lanes].reshape(n // 8, 8, LANES) * (rgrp[s, :, lanes] * SCALE)[None]
            diff = dp[rows, lanes].reshape(n // 8, 8, LANES) - delta[:, lanes][None]
            ds[rows, lanes] = (p * diff).reshape(n, LANES).astype(BF16)
        terms[0, rows, :] = jnp.dot(ds[rows, :], q[...], preferred_element_type=F32)

    def query_terms(j):
        lanes = slice(j * LANES, (j + 1) * LANES)
        rows = jnp.dot(kt[...], ds[:, lanes], preferred_element_type=F32)
        dq[lanes, :] = rows.T.astype(BF16)

    def sum_cross(c, f):
        rows = pl.ds(0, 256 if f >= early else PIECE)
        return remote(x_out.at[c, f, rows], x_in.at[c, f, rows], sx_send.at[c, f], sx_recv.at[c, f], cross)

    def sum_near(c, f, k, n):
        return remote(near_out.at[c, f, k, n - 1], near_in.at[c, f, k, n - 1],
                      sn_send.at[c, f, k, n - 1], sn_recv.at[c, f, k, n - 1], peer(-near_step(f, n)))

    def sum_far(c, f):
        return remote(far_out.at[c, f - 1], far_in.at[c, f - 1],
                      sf_send.at[c, f - 1], sf_recv.at[c, f - 1], peer(-far_step(f)))

    def send_near(c, f, k):
        if k == 0 and f >= early:
            sum_cross(c, f).wait_recv()
        row = 512 * f + 256 * k
        for n in range(1, 4):
            part = terms[c, row + n * PIECE:row + (n + 1) * PIECE, :]
            if k == 0 and f >= early:
                part = part + x_in[c, f, n * PIECE:(n + 1) * PIECE, :].astype(F32)
            near_out[c, f, k, n - 1] = part.astype(BF16)
            sum_near(c, f, k, n).start()

    def near_sum(c, f, k):
        row = 512 * f + 256 * k
        acc = terms[c, row:row + PIECE, :]
        for n in range(1, 4):
            sum_near(c, f, k, n).wait_recv()
            acc = acc + near_in[c, f, k, n - 1].astype(F32)
        return acc

    def send_cross(c, f):
        if f >= early:
            x_out[c, f] = terms[c, 512 * f + 256:512 * f + 512, :].astype(BF16)
        else:
            x_out[c, f, 0:PIECE] = near_sum(c, f, 1).astype(BF16)
        sum_cross(c, f).start()

    def held(c, f):
        acc = near_sum(c, f, 0)
        if f < early:
            sum_cross(c, f).wait_recv()
        return acc + x_in[c, f, 0:PIECE, :].astype(F32)

    def send_far(c, f):
        far_out[c, f - 1] = held(c, f).astype(BF16)
        sum_far(c, f).start()

    def finish(c):
        acc = held(c, 0)
        for f in range(1, fars):
            sum_far(c, f).wait_recv()
            acc = acc + far_in[c, f - 1].astype(F32)
        prm_out[c] = acc.astype(BF16)

    late_groups = list(range(fars - 1, early - 1, -1))
    early_groups = list(range(early - 1, -1, -1))
    far_groups = list(range(fars - 1, 0, -1))

    def both_halves(c, fn):
        for f in late_groups:
            fn(2 * f + 1)
            send_cross(c, f)
        for f in early_groups:
            fn(2 * f + 1)
            send_near(c, f, 1)
        for f in early_groups:
            fn(2 * f)
            send_near(c, f, 0)
        loop(fars, early, lambda f: fn(2 * f))
        fn(last, 128)

    both_halves(V, value_terms)
    delta_terms(last, 128)
    for f in late_groups:
        send_near(V, f, 0)
    loop(0, early, lambda f: near_arrived(V, f, 0), lambda f: delta_terms(2 * f))
    loop(early, fars, lambda f: delta_terms(2 * f))
    for f in early_groups:
        send_cross(V, f)
    loop(0, early, lambda f: near_arrived(V, f, 1), lambda f: delta_terms(2 * f + 1))
    loop(early, fars, lambda f: cross_arrived(V, f), lambda f: delta_terms(2 * f + 1))
    delta[...] = jnp.broadcast_to(jnp.sum(delta[...], axis=0, keepdims=True), delta.shape)
    both_halves(K, key_terms)
    own_out[...] = terms[:, 256 * last:256 * last + ALEN, :].astype(BF16)
    own_store = pltpu.make_async_copy(own_out, dkv_a, st_sem.at[0])
    own_store.start()
    for f in far_groups:
        send_far(V, f)
    for s in range(n_keys // 128):
        kt[:, s * 128:(s + 1) * 128] = kv[2 * s:2 * s + 2, 0].reshape(128, HD).T
    query_terms(0)
    query_terms(1)
    for f in late_groups:
        send_near(K, f, 0)
    query_terms(2)
    query_terms(3)
    for f in early_groups:
        send_cross(K, f)
    query_terms(4)
    query_terms(5)
    for h in range(HEADS):
        cols = pl.ds(h * HD, HD)
        pltpu.make_async_copy(dq.at[pl.ds(h * ALEN, ALEN)], dq_a.at[:, cols], st_sem.at[1]).start()
        pltpu.make_async_copy(dq.at[pl.ds(A_ROWS + h * PIECE, PIECE)], dq_p.at[:, cols], st_sem.at[1]).start()
    for f in far_groups:
        send_far(K, f)
    finish(V)
    finish(K)
    prompt_store = pltpu.make_async_copy(prm_out, dkv_p, st_sem.at[2])
    prompt_store.start()

    for c in range(2):
        for f in range(fars):
            for n in range(4 if f >= early else 1):
                to_cross(c, f, n).wait_send()
            for k in range(1 if f >= early else 2):
                for n in range(1, 4):
                    to_near(c, f, k, n).wait_send()
                    sum_near(c, f, k, n).wait_send()
            sum_cross(c, f).wait_send()
            if f:
                to_far(c, f).wait_send()
                sum_far(c, f).wait_send()
    own_store.wait()
    pltpu.make_async_copy(dq, dq, st_sem.at[1]).wait()
    prompt_store.wait()


def deliver(*refs):
    count = len(refs) // 3
    loads, stores = refs[-2:]
    ins, outs, held = refs[:count], refs[count:2 * count], refs[2 * count:3 * count]
    for i in range(count):
        pltpu.make_async_copy(ins[i], held[i], loads.at[i]).start()
    for i in range(count):
        pltpu.make_async_copy(ins[i], held[i], loads.at[i]).wait()
        pltpu.make_async_copy(held[i], outs[i], stores.at[i]).start()
    for i in range(count):
        pltpu.make_async_copy(held[i], outs[i], stores.at[i]).wait()


def per_device(nz, q_ans, kv_ans, q_prompt, kv_prompt, dout_ans, dout_prompt, ans_len, prompt_len):
    fars = nz // 4
    groups = 2 * fars + 1
    n_keys = 512 * fars + 128
    any_spec = pl.BlockSpec(memory_space=pl.ANY)
    smem = pl.BlockSpec(memory_space=pltpu.SMEM)
    dma, vm = pltpu.SemaphoreType.DMA, pltpu.VMEM
    out_shape = tuple(jax.ShapeDtypeStruct(a.shape, BF16) for a in (q_ans, kv_ans, q_prompt, kv_prompt))
    results = pl.pallas_call(
        functools.partial(kernel, nz),
        out_shape=out_shape,
        in_specs=[smem, smem] + [any_spec] * 6,
        out_specs=(any_spec,) * 4,
        scratch_shapes=[
            vm((n_keys // PIECE, 2, PIECE, HD), BF16),
            vm((HD, n_keys), BF16),
            vm((ROWS, HD), BF16),
            vm((ROWS, HD), BF16),
            vm((n_keys, ROWS), F32),
            vm((n_keys, ROWS), F32),
            vm((n_keys, ROWS), BF16),
            vm((8, ROWS), F32),
            vm((8, ROWS), F32),
            vm((groups, 8, ROWS), F32),
            vm((groups, 8, ROWS), F32),
            vm((8, ROWS), F32),
            vm((2, n_keys, HD), F32),
            vm((ROWS, HD), BF16),
            vm((2, ALEN, HD), BF16),
            vm((2, PIECE, HD), BF16),
            vm((2, fars, 256, HD), BF16), vm((2, fars, 256, HD), BF16),
            vm((2, fars, 2, 3, PIECE, HD), BF16), vm((2, fars, 2, 3, PIECE, HD), BF16),
            vm((2, fars - 1, PIECE, HD), BF16), vm((2, fars - 1, PIECE, HD), BF16),
            dma((5,)), dma((3,)),
            dma((2, fars)), dma((2, fars)), dma((2, fars, 2, 4)), dma((2, fars, 2, 4)),
            dma((2, fars, 4)), dma((2, fars, 4)),
            dma((2, fars - 1)), dma((2, fars - 1)), dma((2, fars, 2, 3)), dma((2, fars, 2, 3)),
            dma((2, fars)), dma((2, fars)),
        ],
        compiler_params=pltpu.CompilerParams(
            collective_id=0, has_side_effects=True, vmem_limit_bytes=58 * 1024 * 1024),
    )(ans_len, prompt_len, q_ans, kv_ans, q_prompt, kv_prompt, dout_ans, dout_prompt)
    return pl.pallas_call(
        deliver, out_shape=out_shape, in_specs=[any_spec] * 4, out_specs=(any_spec,) * 4,
        scratch_shapes=[vm(a.shape, BF16) for a in out_shape] + [dma((4,)), dma((4,))],
    )(*results)


def solution(mesh):
    in_specs = (
        P(("group", "ans"), "tp"),
        P(None, ("group", "ans"), "tp"),
        P(("group", "ans"), "tp"),
        P(None, ("group", "ans"), "tp"),
        P(("group", "ans"), "tp"),
        P(("group", "ans"), "tp"),
        P(("group", "ans")),
        P("group"),
    )
    out_specs = (
        P(("group", "ans"), "tp"),
        P(None, ("group", "ans"), "tp"),
        P(("group", "ans"), "tp"),
        P(None, ("group", "ans"), "tp"),
    )
    return jax.shard_map(
        functools.partial(per_device, mesh.shape["ans"] // 2), mesh=mesh,
        in_specs=in_specs, out_specs=out_specs, check_vma=False)
```

```python
import functools
import math

import jax
import jax.numpy as jnp
from jax import lax
from jax.experimental import pallas as pl
from jax.experimental.pallas import tpu as pltpu
from jax.sharding import PartitionSpec as P

MESH = pl.DeviceIdType.MESH
F32, BF16 = jnp.float32, jnp.bfloat16
HD = 128
HEADS = 8
ALEN = 128
PIECE = 64
A_ROWS = HEADS * ALEN
P_ROWS = HEADS * PIECE
ROWS = A_ROWS + P_ROWS
LANES = 256
CHUNKS = ROWS // LANES
SCALE = 1.0 / math.sqrt(HD)
COEF = SCALE * math.log2(math.e)
NEG = -1e30
NT = (((1,), (1,)), ((), ()))


def far_step(f):
    return 4 * f + f % 2


def near_step(f, n):
    return (0, 1, -1, 2 - 4 * (f % 2))[n]


def kernel(nz, ans_len, prompt_len, q_a, kv_a, q_p, kv_p, g_a, g_p,
           dq_a, dkv_a, dq_p, dkv_p,
           kv, kt, q, g, e, dp, ds, pbuf, mrun, tot, mgrp, rgrp, delta, terms,
           dq, own_out, prm_out,
           x_out, x_in, near_out, near_in, far_out, far_in,
           ld_sem, st_sem, gf_send, gf_recv, gn_send, gn_recv, gx_send, gx_recv,
           sf_send, sf_recv, sn_send, sn_recv, sx_send, sx_recv):
    fars = nz // 4
    last = 2 * fars
    early = fars // 2
    n_keys = 256 * last + 128
    alen = ans_len[0]
    plen = prompt_len[0]
    me = lax.axis_index("ans")
    side = 1 - 2 * (lax.axis_index("group") % 2)
    par = me // nz
    z = me % nz
    cross = {"ans": (1 - par) * nz + z}

    def along(step):
        return (z + side * step + 4 * nz) & (nz - 1)

    places = {step: par * nz + along(step) for step in range(nz)}

    def peer(step):
        return {"ans": places[step % nz] if isinstance(step, int) else par * nz + along(step)}

    barrier = pltpu.get_barrier_semaphore()
    steps = {n % nz for n in (1, -1, 2, -2)}
    for f in range(1, fars):
        steps |= {far_step(f) % nz, -far_step(f) % nz}
    steps = sorted(steps)
    for other in [peer(step) for step in steps] + [cross]:
        pl.semaphore_signal(barrier, inc=1, device_id=other, device_id_type=MESH)

    loads = [pltpu.make_async_copy(kv_p, kv.at[0], ld_sem.at[2])]
    for i in range(2):
        rows = pl.ds(i * PIECE, PIECE)
        loads.append(pltpu.make_async_copy(kv_a.at[:, rows], kv.at[4 * last + i], ld_sem.at[3 + i]))
    for load in loads:
        load.start()
    for h in range(HEADS):
        cols = pl.ds(h * HD, HD)
        pltpu.make_async_copy(q_a.at[:, cols], q.at[pl.ds(h * ALEN, ALEN)], ld_sem.at[0]).start()
        pltpu.make_async_copy(q_p.at[:, cols], q.at[pl.ds(A_ROWS + h * PIECE, PIECE)], ld_sem.at[0]).start()
        pltpu.make_async_copy(g_a.at[:, cols], g.at[pl.ds(h * ALEN, ALEN)], ld_sem.at[1]).start()
        pltpu.make_async_copy(g_p.at[:, cols], g.at[pl.ds(A_ROWS + h * PIECE, PIECE)], ld_sem.at[1]).start()

    pl.semaphore_wait(barrier, len(steps) + 1)

    def remote(src, dst, send, recv, device):
        return pltpu.make_async_remote_copy(
            src_ref=src, dst_ref=dst, send_sem=send, recv_sem=recv,
            device_id=device, device_id_type=MESH)

    def to_far(f):
        return remote(kv_p, kv.at[8 * f], gf_send.at[f], gf_recv.at[f], peer(far_step(f)))

    def to_near(f, k, n, src=None):
        return remote(kv.at[8 * f + 4 * k] if src is None else src, kv.at[8 * f + 4 * k + n],
                      gn_send.at[f, k, n], gn_recv.at[f, k, n], peer(near_step(f, n)))

    def to_cross(f, n, src=None):
        return remote(kv.at[8 * f + n] if src is None else src, kv.at[8 * f + 4 + n],
                      gx_send.at[f, n], gx_recv.at[f, n], cross)

    def spread_cross(f):
        to_cross(f, 0).wait_recv()
        for n in range(1, 4):
            to_near(f, 1, n).start()

    def near_arrived(f, k):
        for n in range(1, 4):
            to_near(f, k, n).wait_recv()

    def near_to_cross(f):
        for n in range(1, 4):
            to_near(f, 0, n).wait_recv()
            to_cross(f, n).start()

    def cross_arrived(f):
        for n in range(4):
            to_cross(f, n).wait_recv()

    K, V = 0, 1
    for f in range(1, fars):
        to_far(f).start()
    to_cross(0, 0, kv_p).start()
    for n in range(1, 4):
        to_near(0, 0, n, kv_p).start()

    pltpu.make_async_copy(q, q, ld_sem.at[0]).wait()
    pltpu.make_async_copy(g, g, ld_sem.at[1]).wait()
    for load in loads:
        load.wait()
    tok = lax.broadcasted_iota(jnp.int32, (A_ROWS, HD), 0) & (ALEN - 1)
    g[0:A_ROWS] = jnp.where(tok < alen, g[0:A_ROWS], jnp.zeros((), BF16))
    tok = me * PIECE + (lax.broadcasted_iota(jnp.int32, (P_ROWS, HD), 0) & (PIECE - 1))
    g[A_ROWS:ROWS] = jnp.where(tok < plen, g[A_ROWS:ROWS], jnp.zeros((), BF16))

    def rows_of(s):
        return pl.multiple_of(s * 256, 256) if not isinstance(s, int) else s * 256

    def limits(j):
        lane = lax.broadcasted_iota(jnp.int32, (1, LANES), 1)
        if j * LANES < A_ROWS:
            return jnp.zeros((1, LANES), jnp.int32) + (plen - 1), lane & (ALEN - 1)
        pos = me * PIECE + (lane & (PIECE - 1))
        return jnp.minimum(pos, plen - 1), jnp.full((1, LANES), -1, jnp.int32)

    def score_group(s, bases, own=False):
        n = PIECE * len(bases) + (ALEN if own else 0)
        rows = pl.ds(rows_of(s), n)
        slots = pl.ds(4 * s, n // PIECE)
        keys = kv[slots, 0].reshape(n, HD)
        values = kv[slots, 1].reshape(n, HD)
        for j in range(CHUNKS):
            lanes = slice(j * LANES, (j + 1) * LANES)
            lim, lim_own = limits(j)
            raw = lax.dot_general(keys, q[lanes, :], NT, preferred_element_type=F32)
            parts = []
            for b, base in enumerate(bases):
                pos = base + lax.broadcasted_iota(jnp.int32, (PIECE, LANES), 0)
                parts.append(jnp.where(pos <= lim, raw[b * PIECE:(b + 1) * PIECE], NEG))
            if own:
                pos = lax.broadcasted_iota(jnp.int32, (ALEN, LANES), 0)
                parts.append(jnp.where(pos <= lim_own, raw[n - ALEN:n], NEG))
            raw = jnp.concatenate(parts, 0).reshape(n // 8, 8, LANES)
            high = jnp.max(raw, axis=0)
            if own:
                new = high
            else:
                old = mrun[:, lanes]
                new = jnp.maximum(old, high)
            ex = jnp.exp2((raw - new[None]) * COEF)
            part = jnp.sum(ex, axis=0)
            if own:
                tot[:, lanes] = part
            else:
                tot[:, lanes] = tot[:, lanes] * jnp.exp2((old - new) * COEF) + part
            mrun[:, lanes] = new
            mgrp[s, :, lanes] = new
            e[rows, lanes] = ex.reshape(n, LANES)
            dp[rows, lanes] = lax.dot_general(values, g[lanes, :], NT, preferred_element_type=F32)

    def bases(f, k):
        half = par if k == 0 else 1 - par
        return [(half * nz + along(-(near_step(f, n) + far_step(f)))) * PIECE for n in range(4)]

    def loop(first, stop, *steps):
        def body(i, carry):
            f = first + i if stop >= first else first - 1 - i
            for step in steps:
                step(f)
            return carry
        lax.fori_loop(0, abs(stop - first), body, 0)

    def loop(first, stop, *steps):
        def body(i, carry):
            f = first + i if stop >= first else first - 1 - i
            for step in steps:
                step(f)
            return carry
        lax.fori_loop(0, abs(stop - first), body, 0)

    def score(f, k):
        score_group(2 * f + k, bases(f, k))

    score_group(last, [], True)
    for f in range(1, fars):
        to_far(f).wait_recv()
        to_cross(f, 0).start()
        for n in range(1, 4):
            to_near(f, 0, n).start()
    for f in range(early):
        spread_cross(f)
        near_arrived(f, 0)
        score(f, 0)
    for f in range(early, fars):
        near_to_cross(f)
    loop(early, fars, lambda f: score(f, 0))
    loop(0, early, lambda f: near_arrived(f, 1), lambda f: score(f, 1))
    loop(early, fars, lambda f: cross_arrived(f), lambda f: score(f, 1))

    m8 = mrun[...]
    top = jnp.max(m8, axis=0, keepdims=True)
    total = jnp.sum(tot[...] * jnp.exp2((m8 - top) * COEF), axis=0, keepdims=True)
    inv = 1.0 / total
    for s in range(last + 1):
        rgrp[s] = jnp.exp2((mgrp[s] - top) * COEF) * inv
    delta[...] = jnp.zeros_like(delta)

    def value_terms(s, n=256):
        rows = pl.ds(rows_of(s), n)
        for j in range(CHUNKS):
            lanes = slice(j * LANES, (j + 1) * LANES)
            p = e[rows, lanes].reshape(n // 8, 8, LANES) * rgrp[s, :, lanes][None]
            pb = p.reshape(n, LANES).astype(BF16)
            pbuf[0:n, lanes] = pb
            prod = pb.astype(F32) * dp[rows, lanes]
            delta[:, lanes] += jnp.sum(prod.reshape(n // 8, 8, LANES), axis=0)
        terms[1, rows, :] = jnp.dot(pbuf[0:n], g[...], preferred_element_type=F32)

    def key_terms(s, n=256):
        rows = pl.ds(rows_of(s), n)
        for j in range(CHUNKS):
            lanes = slice(j * LANES, (j + 1) * LANES)
            p = e[rows, lanes].reshape(n // 8, 8, LANES) * (rgrp[s, :, lanes] * SCALE)[None]
            diff = dp[rows, lanes].reshape(n // 8, 8, LANES) - delta[:, lanes][None]
            ds[rows, lanes] = (p * diff).reshape(n, LANES).astype(BF16)
        terms[0, rows, :] = jnp.dot(ds[rows, :], q[...], preferred_element_type=F32)

    def query_terms(j):
        lanes = slice(j * LANES, (j + 1) * LANES)
        rows = jnp.dot(kt[...], ds[:, lanes], preferred_element_type=F32)
        dq[lanes, :] = rows.T.astype(BF16)

    def sum_cross(c, f):
        rows = pl.ds(0, 256 if f >= early else PIECE)
        return remote(x_out.at[c, f, rows], x_in.at[c, f, rows], sx_send.at[c, f], sx_recv.at[c, f], cross)

    def sum_near(c, f, k, n):
        return remote(near_out.at[c, f, k, n - 1], near_in.at[c, f, k, n - 1],
                      sn_send.at[c, f, k, n - 1], sn_recv.at[c, f, k, n - 1], peer(-near_step(f, n)))

    def sum_far(c, f):
        return remote(far_out.at[c, f - 1], far_in.at[c, f - 1],
                      sf_send.at[c, f - 1], sf_recv.at[c, f - 1], peer(-far_step(f)))

    def send_near(c, f, k):
        if k == 0 and f >= early:
            sum_cross(c, f).wait_recv()
        row = 512 * f + 256 * k
        for n in range(1, 4):
            part = terms[c, row + n * PIECE:row + (n + 1) * PIECE, :]
            if k == 0 and f >= early:
                part = part + x_in[c, f, n * PIECE:(n + 1) * PIECE, :].astype(F32)
            near_out[c, f, k, n - 1] = part.astype(BF16)
            sum_near(c, f, k, n).start()

    def near_sum(c, f, k):
        row = 512 * f + 256 * k
        acc = terms[c, row:row + PIECE, :]
        for n in range(1, 4):
            sum_near(c, f, k, n).wait_recv()
            acc = acc + near_in[c, f, k, n - 1].astype(F32)
        return acc

    def send_cross(c, f):
        if f >= early:
            x_out[c, f] = terms[c, 512 * f + 256:512 * f + 512, :].astype(BF16)
        else:
            x_out[c, f, 0:PIECE] = near_sum(c, f, 1).astype(BF16)
        sum_cross(c, f).start()

    def held(c, f):
        acc = near_sum(c, f, 0)
        if f < early:
            sum_cross(c, f).wait_recv()
        return acc + x_in[c, f, 0:PIECE, :].astype(F32)

    def send_far(c, f):
        far_out[c, f - 1] = held(c, f).astype(BF16)
        sum_far(c, f).start()

    def finish(c):
        acc = held(c, 0)
        for f in range(1, fars):
            sum_far(c, f).wait_recv()
            acc = acc + far_in[c, f - 1].astype(F32)
        prm_out[c] = acc.astype(BF16)

    late_groups = list(range(fars - 1, early - 1, -1))
    early_groups = list(range(early - 1, -1, -1))
    far_groups = list(range(fars - 1, 0, -1))

    for f in late_groups:
        value_terms(2 * f + 1)
        send_cross(V, f)
    for f in early_groups:
        value_terms(2 * f + 1)
        send_near(V, f, 1)
    for f in early_groups:
        value_terms(2 * f)
        send_near(V, f, 0)
    loop(fars, early, lambda f: value_terms(2 * f))
    value_terms(last, 128)
    delta[...] = jnp.broadcast_to(jnp.sum(delta[...], axis=0, keepdims=True), delta.shape)
    for f in late_groups:
        key_terms(2 * f + 1)
        send_cross(K, f)
    for f in late_groups:
        send_near(V, f, 0)
    for f in early_groups:
        key_terms(2 * f + 1)
        send_near(K, f, 1)
    for f in early_groups:
        send_cross(V, f)
    for f in early_groups:
        key_terms(2 * f)
        send_near(K, f, 0)
    loop(fars, early, lambda f: key_terms(2 * f))
    for f in late_groups:
        send_near(K, f, 0)
    key_terms(last, 128)
    own_out[...] = terms[:, 256 * last:256 * last + ALEN, :].astype(BF16)
    own_store = pltpu.make_async_copy(own_out, dkv_a, st_sem.at[0])
    own_store.start()
    for f in far_groups:
        send_far(V, f)
    for f in early_groups:
        send_cross(K, f)
    for s in range(n_keys // 128):
        kt[:, s * 128:(s + 1) * 128] = kv[2 * s:2 * s + 2, 0].reshape(128, HD).T
    for j in range(CHUNKS // 2):
        query_terms(j)
    late_far = [f for f in far_groups if f >= early]
    for f in late_far:
        send_far(K, f)
    for j in range(CHUNKS // 2, CHUNKS):
        query_terms(j)
    for f in far_groups:
        if f not in late_far:
            send_far(K, f)
    for h in range(HEADS):
        cols = pl.ds(h * HD, HD)
        pltpu.make_async_copy(dq.at[pl.ds(h * ALEN, ALEN)], dq_a.at[:, cols], st_sem.at[1]).start()
        pltpu.make_async_copy(dq.at[pl.ds(A_ROWS + h * PIECE, PIECE)], dq_p.at[:, cols], st_sem.at[1]).start()

    def sent(c):
        for f in range(fars):
            for k in range(1 if f >= early else 2):
                for n in range(1, 4):
                    sum_near(c, f, k, n).wait_send()
            sum_cross(c, f).wait_send()
            if f:
                sum_far(c, f).wait_send()

    finish(V)
    for f in range(fars):
        for n in range(4 if f >= early else 1):
            to_cross(f, n).wait_send()
        for k in range(1 if f >= early else 2):
            for n in range(1, 4):
                to_near(f, k, n).wait_send()
        if f:
            to_far(f).wait_send()
    sent(V)
    own_store.wait()
    pltpu.make_async_copy(dq, dq, st_sem.at[1]).wait()
    finish(K)
    prompt_store = pltpu.make_async_copy(prm_out, dkv_p, st_sem.at[2])
    prompt_store.start()
    sent(K)
    prompt_store.wait()


def deliver(*refs):
    count = len(refs) // 3
    loads, stores = refs[-2:]
    ins, outs, held = refs[:count], refs[count:2 * count], refs[2 * count:3 * count]
    for i in range(count):
        pltpu.make_async_copy(ins[i], held[i], loads.at[i]).start()
    for i in range(count):
        pltpu.make_async_copy(ins[i], held[i], loads.at[i]).wait()
        pltpu.make_async_copy(held[i], outs[i], stores.at[i]).start()
    for i in range(count):
        pltpu.make_async_copy(held[i], outs[i], stores.at[i]).wait()


def per_device(nz, q_ans, kv_ans, q_prompt, kv_prompt, dout_ans, dout_prompt, ans_len, prompt_len):
    fars = nz // 4
    groups = 2 * fars + 1
    n_keys = 512 * fars + 128
    any_spec = pl.BlockSpec(memory_space=pl.ANY)
    smem = pl.BlockSpec(memory_space=pltpu.SMEM)
    dma, vm = pltpu.SemaphoreType.DMA, pltpu.VMEM
    out_shape = tuple(jax.ShapeDtypeStruct(a.shape, BF16) for a in (q_ans, kv_ans, q_prompt, kv_prompt))
    results = pl.pallas_call(
        functools.partial(kernel, nz),
        out_shape=out_shape,
        in_specs=[smem, smem] + [any_spec] * 6,
        out_specs=(any_spec,) * 4,
        scratch_shapes=[
            vm((n_keys // PIECE, 2, PIECE, HD), BF16),
            vm((HD, n_keys), BF16),
            vm((ROWS, HD), BF16),
            vm((ROWS, HD), BF16),
            vm((n_keys, ROWS), F32),
            vm((n_keys, ROWS), F32),
            vm((n_keys, ROWS), BF16),
            vm((256, ROWS), BF16),
            vm((8, ROWS), F32),
            vm((8, ROWS), F32),
            vm((groups, 8, ROWS), F32),
            vm((groups, 8, ROWS), F32),
            vm((8, ROWS), F32),
            vm((2, n_keys, HD), F32),
            vm((ROWS, HD), BF16),
            vm((2, ALEN, HD), BF16),
            vm((2, PIECE, HD), BF16),
            vm((2, fars, 256, HD), BF16), vm((2, fars, 256, HD), BF16),
            vm((2, fars, 2, 3, PIECE, HD), BF16), vm((2, fars, 2, 3, PIECE, HD), BF16),
            vm((2, fars - 1, PIECE, HD), BF16), vm((2, fars - 1, PIECE, HD), BF16),
            dma((5,)), dma((3,)),
            dma((fars,)), dma((fars,)), dma((fars, 2, 4)), dma((fars, 2, 4)),
            dma((fars, 4)), dma((fars, 4)),
            dma((2, fars - 1)), dma((2, fars - 1)), dma((2, fars, 2, 3)), dma((2, fars, 2, 3)),
            dma((2, fars)), dma((2, fars)),
        ],
        compiler_params=pltpu.CompilerParams(
            collective_id=0, has_side_effects=True, vmem_limit_bytes=58 * 1024 * 1024),
    )(ans_len, prompt_len, q_ans, kv_ans, q_prompt, kv_prompt, dout_ans, dout_prompt)
    return pl.pallas_call(
        deliver, out_shape=out_shape, in_specs=[any_spec] * 4, out_specs=(any_spec,) * 4,
        scratch_shapes=[vm(a.shape, BF16) for a in out_shape] + [dma((4,)), dma((4,))],
    )(*results)


def solution(mesh):
    in_specs = (
        P(("group", "ans"), "tp"),
        P(None, ("group", "ans"), "tp"),
        P(("group", "ans"), "tp"),
        P(None, ("group", "ans"), "tp"),
        P(("group", "ans"), "tp"),
        P(("group", "ans"), "tp"),
        P(("group", "ans")),
        P("group"),
    )
    out_specs = (
        P(("group", "ans"), "tp"),
        P(None, ("group", "ans"), "tp"),
        P(("group", "ans"), "tp"),
        P(None, ("group", "ans"), "tp"),
    )
    return jax.shard_map(
        functools.partial(per_device, mesh.shape["ans"] // 2), mesh=mesh,
        in_specs=in_specs, out_specs=out_specs, check_vma=False)
```

```python
import functools
import math

import jax
import jax.numpy as jnp
from jax import lax
from jax.experimental import pallas as pl
from jax.experimental.pallas import tpu as pltpu
from jax.sharding import PartitionSpec as P

MESH = pl.DeviceIdType.MESH
F32, BF16 = jnp.float32, jnp.bfloat16
HD = 128
HEADS = 8
ALEN = 128
PIECE = 64
A_ROWS = HEADS * ALEN
P_ROWS = HEADS * PIECE
ROWS = A_ROWS + P_ROWS
LANES = 256
CHUNKS = ROWS // LANES
SCALE = 1.0 / math.sqrt(HD)
COEF = SCALE * math.log2(math.e)
NEG = -1e30
NT = (((1,), (1,)), ((), ()))


def far_step(f):
    return 4 * f + f % 2


def near_step(f, n):
    return (0, 1, -1, 2 - 4 * (f % 2))[n]


def kernel(nz, ans_len, prompt_len, q_a, kv_a, q_p, kv_p, g_a, g_p,
           dq_a, dkv_a, dq_p, dkv_p,
           kv, kt, q, g, e, dp, ds, pbuf, mrun, tot, mgrp, rgrp, delta, terms,
           dq, own_out, prm_out,
           near_out, near_in, far_out, far_in,
           ld_sem, st_sem, gf_send, gf_recv, gn_send, gn_recv, sf_send, sf_recv, sn_send, sn_recv):
    fars = nz // 4
    last = 2 * fars
    n_keys = 256 * last + 128
    alen = ans_len[0]
    plen = prompt_len[0]
    me = lax.axis_index("ans")
    side = 1 - 2 * (lax.axis_index("group") % 2)
    par = me // nz
    z = me % nz

    def along(step):
        return (z + side * step + 4 * nz) & (nz - 1)

    places = {step: along(step) for step in range(nz)}

    def peer(step, k=0):
        there = places[step % nz] if isinstance(step, int) else along(step)
        return {"ans": (1 - par if k else par) * nz + there}

    far_steps = set()
    for f in range(1, fars):
        far_steps |= {far_step(f) % nz, -far_step(f) % nz}
    others = [peer(step) for step in sorted(far_steps | {n % nz for n in (1, -1, 2, -2)})]
    others += [peer(step, 1) for step in sorted(far_steps | {0})]
    barrier = pltpu.get_barrier_semaphore()
    for other in others:
        pl.semaphore_signal(barrier, inc=1, device_id=other, device_id_type=MESH)

    loads = [pltpu.make_async_copy(kv_p, kv.at[0], ld_sem.at[2])]
    for i in range(2):
        rows = pl.ds(i * PIECE, PIECE)
        loads.append(pltpu.make_async_copy(kv_a.at[:, rows], kv.at[4 * last + i], ld_sem.at[3 + i]))
    for load in loads:
        load.start()
    for h in range(HEADS):
        cols = pl.ds(h * HD, HD)
        pltpu.make_async_copy(q_a.at[:, cols], q.at[pl.ds(h * ALEN, ALEN)], ld_sem.at[0]).start()
        pltpu.make_async_copy(q_p.at[:, cols], q.at[pl.ds(A_ROWS + h * PIECE, PIECE)], ld_sem.at[0]).start()
        pltpu.make_async_copy(g_a.at[:, cols], g.at[pl.ds(h * ALEN, ALEN)], ld_sem.at[1]).start()
        pltpu.make_async_copy(g_p.at[:, cols], g.at[pl.ds(A_ROWS + h * PIECE, PIECE)], ld_sem.at[1]).start()

    pl.semaphore_wait(barrier, len(others))

    def remote(src, dst, send, recv, device):
        return pltpu.make_async_remote_copy(
            src_ref=src, dst_ref=dst, send_sem=send, recv_sem=recv,
            device_id=device, device_id_type=MESH)

    far_pairs = [(0, 1)] + [(f, k) for f in range(1, fars) for k in range(2)]

    def to_far(f, k):
        return remote(kv_p, kv.at[8 * f + k], gf_send.at[f, k], gf_recv.at[f, k], peer(far_step(f), k))

    def to_near(f, n):
        return remote(kv.at[pl.ds(8 * f, 2)], kv.at[pl.ds(8 * f + 2 * n, 2)],
                      gn_send.at[f, n], gn_recv.at[f, n], peer(near_step(f, n)))

    K, V = 0, 1
    for f, k in far_pairs:
        to_far(f, k).start()

    pltpu.make_async_copy(q, q, ld_sem.at[0]).wait()
    pltpu.make_async_copy(g, g, ld_sem.at[1]).wait()
    for load in loads:
        load.wait()
    tok = lax.broadcasted_iota(jnp.int32, (A_ROWS, HD), 0) & (ALEN - 1)
    g[0:A_ROWS] = jnp.where(tok < alen, g[0:A_ROWS], jnp.zeros((), BF16))
    tok = me * PIECE + (lax.broadcasted_iota(jnp.int32, (P_ROWS, HD), 0) & (PIECE - 1))
    g[A_ROWS:ROWS] = jnp.where(tok < plen, g[A_ROWS:ROWS], jnp.zeros((), BF16))

    def rows_of(s):
        return pl.multiple_of(s * 256, 256) if not isinstance(s, int) else s * 256

    def limits(j):
        lane = lax.broadcasted_iota(jnp.int32, (1, LANES), 1)
        if j * LANES < A_ROWS:
            return jnp.zeros((1, LANES), jnp.int32) + (plen - 1), lane & (ALEN - 1)
        pos = me * PIECE + (lane & (PIECE - 1))
        return jnp.minimum(pos, plen - 1), jnp.full((1, LANES), -1, jnp.int32)

    def score_group(s, bases, own=False):
        n = PIECE * len(bases) + (ALEN if own else 0)
        rows = pl.ds(rows_of(s), n)
        slots = pl.ds(4 * s, n // PIECE)
        keys = kv[slots, 0].reshape(n, HD)
        values = kv[slots, 1].reshape(n, HD)
        for j in range(CHUNKS):
            lanes = slice(j * LANES, (j + 1) * LANES)
            lim, lim_own = limits(j)
            raw = lax.dot_general(keys, q[lanes, :], NT, preferred_element_type=F32)
            parts = []
            for b, base in enumerate(bases):
                pos = base + lax.broadcasted_iota(jnp.int32, (PIECE, LANES), 0)
                parts.append(jnp.where(pos <= lim, raw[b * PIECE:(b + 1) * PIECE], NEG))
            if own:
                pos = lax.broadcasted_iota(jnp.int32, (ALEN, LANES), 0)
                parts.append(jnp.where(pos <= lim_own, raw[n - ALEN:n], NEG))
            raw = jnp.concatenate(parts, 0).reshape(n // 8, 8, LANES)
            high = jnp.max(raw, axis=0)
            if own:
                new = high
            else:
                old = mrun[:, lanes]
                new = jnp.maximum(old, high)
            ex = jnp.exp2((raw - new[None]) * COEF)
            part = jnp.sum(ex, axis=0)
            if own:
                tot[:, lanes] = part
            else:
                tot[:, lanes] = tot[:, lanes] * jnp.exp2((old - new) * COEF) + part
            mrun[:, lanes] = new
            mgrp[s, :, lanes] = new
            e[rows, lanes] = ex.reshape(n, LANES)
            dp[rows, lanes] = lax.dot_general(values, g[lanes, :], NT, preferred_element_type=F32)

    def bases(f, half):
        there = [along(-(near_step(f, 2 * half + i) + far_step(f))) for i in range(2)]
        return [((1 - par if k else par) * nz + there[i]) * PIECE for i in range(2) for k in range(2)]

    def loop(first, stop, *steps):
        def body(i, carry):
            f = first + i if stop >= first else first - 1 - i
            for step in steps:
                step(f)
            return carry
        lax.fori_loop(0, abs(stop - first), body, 0)

    def loop(first, stop, *steps):
        def body(i, carry):
            f = first + i if stop >= first else first - 1 - i
            for step in steps:
                step(f)
            return carry
        lax.fori_loop(0, abs(stop - first), body, 0)

    def score(f, k):
        score_group(2 * f + k, bases(f, k))

    score_group(last, [], True)
    for f in range(fars):
        for k in range(2):
            if (f, k) in far_pairs:
                to_far(f, k).wait_recv()
        for n in range(1, 4):
            to_near(f, n).start()

    def score_far(f):
        to_near(f, 1).wait_recv()
        score(f, 0)
        to_near(f, 2).wait_recv()
        to_near(f, 3).wait_recv()
        score(f, 1)

    loop(0, fars, score_far)

    m8 = mrun[...]
    top = jnp.max(m8, axis=0, keepdims=True)
    total = jnp.sum(tot[...] * jnp.exp2((m8 - top) * COEF), axis=0, keepdims=True)
    inv = 1.0 / total
    for s in range(last + 1):
        rgrp[s] = jnp.exp2((mgrp[s] - top) * COEF) * inv
    delta[...] = jnp.zeros_like(delta)

    def value_terms(s, n=256):
        rows = pl.ds(rows_of(s), n)
        for j in range(CHUNKS):
            lanes = slice(j * LANES, (j + 1) * LANES)
            p = e[rows, lanes].reshape(n // 8, 8, LANES) * rgrp[s, :, lanes][None]
            pb = p.reshape(n, LANES).astype(BF16)
            pbuf[0:n, lanes] = pb
            prod = pb.astype(F32) * dp[rows, lanes]
            delta[:, lanes] += jnp.sum(prod.reshape(n // 8, 8, LANES), axis=0)
        terms[1, rows, :] = jnp.dot(pbuf[0:n], g[...], preferred_element_type=F32)

    def key_terms(s, n=256):
        rows = pl.ds(rows_of(s), n)
        for j in range(CHUNKS):
            lanes = slice(j * LANES, (j + 1) * LANES)
            p = e[rows, lanes].reshape(n // 8, 8, LANES) * (rgrp[s, :, lanes] * SCALE)[None]
            diff = dp[rows, lanes].reshape(n // 8, 8, LANES) - delta[:, lanes][None]
            ds[rows, lanes] = (p * diff).reshape(n, LANES).astype(BF16)
        terms[0, rows, :] = jnp.dot(ds[rows, :], q[...], preferred_element_type=F32)

    def query_terms(j):
        lanes = slice(j * LANES, (j + 1) * LANES)
        rows = jnp.dot(kt[...], ds[:, lanes], preferred_element_type=F32)
        dq[lanes, :] = rows.T.astype(BF16)

    def sum_near(c, f, n):
        return remote(near_out.at[c, f, n - 1], near_in.at[c, f, n - 1],
                      sn_send.at[c, f, n - 1], sn_recv.at[c, f, n - 1], peer(-near_step(f, n)))

    def sum_far(c, f, k):
        return remote(far_out.at[c, f, k], far_in.at[c, f, k],
                      sf_send.at[c, f, k], sf_recv.at[c, f, k], peer(-far_step(f), k))

    def send_near(c, f):
        for n in range(1, 4):
            row = pl.multiple_of(512 * f + 128 * n, 128)
            near_out[c, f, n - 1] = terms[c, pl.ds(row, 128), :].astype(BF16)
            sum_near(c, f, n).start()

    def near_sum(c, f):
        acc = terms[c, 512 * f:512 * f + 128, :]
        for n in range(1, 4):
            sum_near(c, f, n).wait_recv()
            acc = acc + near_in[c, f, n - 1].astype(F32)
        return acc

    def send_far(c, f):
        acc = near_sum(c, f)
        for k in range(2):
            if (f, k) in far_pairs:
                far_out[c, f, k] = acc[k * PIECE:(k + 1) * PIECE].astype(BF16)
                sum_far(c, f, k).start()
        if f == 0:
            terms[c, 0:PIECE, :] = acc[0:PIECE]

    def finish(c):
        acc = terms[c, 0:PIECE, :]
        for f, k in far_pairs:
            sum_far(c, f, k).wait_recv()
            acc = acc + far_in[c, f, k].astype(F32)
        prm_out[c] = acc.astype(BF16)

    def terms_of(c, fn):
        def both(f):
            fn(2 * f)
            fn(2 * f + 1)
            send_near(c, f)
        return both

    loop(fars, 0, terms_of(V, value_terms))
    value_terms(last, 128)
    delta[...] = jnp.broadcast_to(jnp.sum(delta[...], axis=0, keepdims=True), delta.shape)
    loop(fars, fars // 2, terms_of(K, key_terms))
    for f in range(fars - 1, fars // 2 - 1, -1):
        send_far(V, f)
    loop(fars // 2, 0, terms_of(K, key_terms))
    for f in range(fars // 2 - 1, -1, -1):
        send_far(V, f)
    key_terms(last, 128)
    own_out[...] = terms[:, 256 * last:256 * last + ALEN, :].astype(BF16)
    own_store = pltpu.make_async_copy(own_out, dkv_a, st_sem.at[0])
    own_store.start()
    for s in range(n_keys // 128):
        kt[:, s * 128:(s + 1) * 128] = kv[2 * s:2 * s + 2, 0].reshape(128, HD).T
    for j in range(CHUNKS // 2):
        query_terms(j)
    for f in range(fars - 1, fars // 2 - 1, -1):
        send_far(K, f)
    for j in range(CHUNKS // 2, CHUNKS):
        query_terms(j)
    for f in range(fars // 2 - 1, -1, -1):
        send_far(K, f)
    for h in range(HEADS):
        cols = pl.ds(h * HD, HD)
        pltpu.make_async_copy(dq.at[pl.ds(h * ALEN, ALEN)], dq_a.at[:, cols], st_sem.at[1]).start()
        pltpu.make_async_copy(dq.at[pl.ds(A_ROWS + h * PIECE, PIECE)], dq_p.at[:, cols], st_sem.at[1]).start()

    def sent(c):
        for f in range(fars):
            for n in range(1, 4):
                sum_near(c, f, n).wait_send()
        for f, k in far_pairs:
            sum_far(c, f, k).wait_send()

    for f in range(fars):
        for n in range(1, 4):
            to_near(f, n).wait_send()
    for f, k in far_pairs:
        to_far(f, k).wait_send()
    finish(V)
    sent(V)
    own_store.wait()
    pltpu.make_async_copy(dq, dq, st_sem.at[1]).wait()
    finish(K)
    prompt_store = pltpu.make_async_copy(prm_out, dkv_p, st_sem.at[2])
    prompt_store.start()
    sent(K)
    prompt_store.wait()


def deliver(*refs):
    count = len(refs) // 3
    loads, stores = refs[-2:]
    ins, outs, held = refs[:count], refs[count:2 * count], refs[2 * count:3 * count]
    for i in range(count):
        pltpu.make_async_copy(ins[i], held[i], loads.at[i]).start()
    for i in range(count):
        pltpu.make_async_copy(ins[i], held[i], loads.at[i]).wait()
        pltpu.make_async_copy(held[i], outs[i], stores.at[i]).start()
    for i in range(count):
        pltpu.make_async_copy(held[i], outs[i], stores.at[i]).wait()


def per_device(nz, q_ans, kv_ans, q_prompt, kv_prompt, dout_ans, dout_prompt, ans_len, prompt_len):
    fars = nz // 4
    groups = 2 * fars + 1
    n_keys = 512 * fars + 128
    any_spec = pl.BlockSpec(memory_space=pl.ANY)
    smem = pl.BlockSpec(memory_space=pltpu.SMEM)
    dma, vm = pltpu.SemaphoreType.DMA, pltpu.VMEM
    out_shape = tuple(jax.ShapeDtypeStruct(a.shape, BF16) for a in (q_ans, kv_ans, q_prompt, kv_prompt))
    results = pl.pallas_call(
        functools.partial(kernel, nz),
        out_shape=out_shape,
        in_specs=[smem, smem] + [any_spec] * 6,
        out_specs=(any_spec,) * 4,
        scratch_shapes=[
            vm((n_keys // PIECE, 2, PIECE, HD), BF16),
            vm((HD, n_keys), BF16),
            vm((ROWS, HD), BF16),
            vm((ROWS, HD), BF16),
            vm((n_keys, ROWS), F32),
            vm((n_keys, ROWS), F32),
            vm((n_keys, ROWS), BF16),
            vm((256, ROWS), BF16),
            vm((8, ROWS), F32),
            vm((8, ROWS), F32),
            vm((groups, 8, ROWS), F32),
            vm((groups, 8, ROWS), F32),
            vm((8, ROWS), F32),
            vm((2, n_keys, HD), F32),
            vm((ROWS, HD), BF16),
            vm((2, ALEN, HD), BF16),
            vm((2, PIECE, HD), BF16),
            vm((2, fars, 3, 2 * PIECE, HD), BF16), vm((2, fars, 3, 2 * PIECE, HD), BF16),
            vm((2, fars, 2, PIECE, HD), BF16), vm((2, fars, 2, PIECE, HD), BF16),
            dma((5,)), dma((3,)),
            dma((fars, 2)), dma((fars, 2)), dma((fars, 4)), dma((fars, 4)),
            dma((2, fars, 2)), dma((2, fars, 2)), dma((2, fars, 3)), dma((2, fars, 3)),
        ],
        compiler_params=pltpu.CompilerParams(
            collective_id=0, has_side_effects=True, vmem_limit_bytes=58 * 1024 * 1024),
    )(ans_len, prompt_len, q_ans, kv_ans, q_prompt, kv_prompt, dout_ans, dout_prompt)
    return pl.pallas_call(
        deliver, out_shape=out_shape, in_specs=[any_spec] * 4, out_specs=(any_spec,) * 4,
        scratch_shapes=[vm(a.shape, BF16) for a in out_shape] + [dma((4,)), dma((4,))],
    )(*results)


def solution(mesh):
    in_specs = (
        P(("group", "ans"), "tp"),
        P(None, ("group", "ans"), "tp"),
        P(("group", "ans"), "tp"),
        P(None, ("group", "ans"), "tp"),
        P(("group", "ans"), "tp"),
        P(("group", "ans"), "tp"),
        P(("group", "ans")),
        P("group"),
    )
    out_specs = (
        P(("group", "ans"), "tp"),
        P(None, ("group", "ans"), "tp"),
        P(("group", "ans"), "tp"),
        P(None, ("group", "ans"), "tp"),
    )
    return jax.shard_map(
        functools.partial(per_device, mesh.shape["ans"] // 2), mesh=mesh,
        in_specs=in_specs, out_specs=out_specs, check_vma=False)
```

```python
import functools
import math

import jax
import jax.numpy as jnp
from jax import lax
from jax.experimental import pallas as pl
from jax.experimental.pallas import tpu as pltpu
from jax.sharding import PartitionSpec as P

MESH = pl.DeviceIdType.MESH
F32, BF16 = jnp.float32, jnp.bfloat16
HD = 128
HEADS = 8
ALEN = 128
PIECE = 64
A_ROWS = HEADS * ALEN
P_ROWS = HEADS * PIECE
ROWS = A_ROWS + P_ROWS
LANES = 256
CHUNKS = ROWS // LANES
SCALE = 1.0 / math.sqrt(HD)
COEF = SCALE * math.log2(math.e)
NEG = -1e30
NT = (((1,), (1,)), ((), ()))


def leans(f):
    return (f + 1) // 2 % 2


def far_step(f):
    return 4 * f + leans(f)


def near_step(f, n):
    return (0, 1, -1, 2 - 4 * leans(f))[n]


def kernel(nz, ans_len, prompt_len, q_a, kv_a, q_p, kv_p, g_a, g_p,
           dq_a, dkv_a, dq_p, dkv_p,
           kv, kt, q, g, e, dp, ds, pbuf, mrun, tot, mgrp, rgrp, delta, terms,
           dq, own_out, prm_out,
           x_out, x_in, near_out, near_in, far_out, far_in,
           ld_sem, st_sem, gf_send, gf_recv, gn_send, gn_recv, gx_send, gx_recv,
           sf_send, sf_recv, sn_send, sn_recv, sx_send, sx_recv):
    fars = nz // 4
    last = 2 * fars
    early = max(1, fars // 4)
    n_keys = 256 * last + 128
    alen = ans_len[0]
    plen = prompt_len[0]
    me = lax.axis_index("ans")
    side = 1 - 2 * (lax.axis_index("group") % 2)
    par = me // nz
    z = me % nz
    cross = {"ans": (1 - par) * nz + z}

    def along(step):
        return (z + side * step + 4 * nz) & (nz - 1)

    places = {step: par * nz + along(step) for step in range(nz)}

    def peer(step):
        return {"ans": places[step % nz] if isinstance(step, int) else par * nz + along(step)}

    barrier = pltpu.get_barrier_semaphore()
    steps = {n % nz for n in (1, -1, 2, -2)}
    for f in range(1, fars):
        steps |= {far_step(f) % nz, -far_step(f) % nz}
    steps = sorted(steps)
    for other in [peer(step) for step in steps] + [cross]:
        pl.semaphore_signal(barrier, inc=1, device_id=other, device_id_type=MESH)

    loads = [pltpu.make_async_copy(kv_p, kv.at[0], ld_sem.at[2])]
    for i in range(2):
        rows = pl.ds(i * PIECE, PIECE)
        loads.append(pltpu.make_async_copy(kv_a.at[:, rows], kv.at[4 * last + i], ld_sem.at[3 + i]))
    for load in loads:
        load.start()
    for h in range(HEADS):
        cols = pl.ds(h * HD, HD)
        pltpu.make_async_copy(q_a.at[:, cols], q.at[pl.ds(h * ALEN, ALEN)], ld_sem.at[0]).start()
        pltpu.make_async_copy(q_p.at[:, cols], q.at[pl.ds(A_ROWS + h * PIECE, PIECE)], ld_sem.at[0]).start()
        pltpu.make_async_copy(g_a.at[:, cols], g.at[pl.ds(h * ALEN, ALEN)], ld_sem.at[1]).start()
        pltpu.make_async_copy(g_p.at[:, cols], g.at[pl.ds(A_ROWS + h * PIECE, PIECE)], ld_sem.at[1]).start()

    pl.semaphore_wait(barrier, len(steps) + 1)

    def remote(src, dst, send, recv, device):
        return pltpu.make_async_remote_copy(
            src_ref=src, dst_ref=dst, send_sem=send, recv_sem=recv,
            device_id=device, device_id_type=MESH)

    def to_far(f):
        return remote(kv_p, kv.at[8 * f], gf_send.at[f], gf_recv.at[f], peer(far_step(f)))

    def to_near(f, k, n, src=None):
        return remote(kv.at[8 * f + 4 * k] if src is None else src, kv.at[8 * f + 4 * k + n],
                      gn_send.at[f, k, n], gn_recv.at[f, k, n], peer(near_step(f, n)))

    def to_cross(f, n, src=None):
        return remote(kv.at[8 * f + n] if src is None else src, kv.at[8 * f + 4 + n],
                      gx_send.at[f, n], gx_recv.at[f, n], cross)

    def spread_cross(f):
        to_cross(f, 0).wait_recv()
        for n in range(1, 4):
            to_near(f, 1, n).start()

    def near_arrived(f, k):
        for n in range(1, 4):
            to_near(f, k, n).wait_recv()

    def near_to_cross(f):
        for n in range(1, 4):
            to_near(f, 0, n).wait_recv()
            to_cross(f, n).start()

    def cross_arrived(f):
        for n in range(4):
            to_cross(f, n).wait_recv()

    K, V = 0, 1
    for f in range(1, fars):
        to_far(f).start()
    to_cross(0, 0, kv_p).start()
    for n in range(1, 4):
        to_near(0, 0, n, kv_p).start()

    pltpu.make_async_copy(q, q, ld_sem.at[0]).wait()
    pltpu.make_async_copy(g, g, ld_sem.at[1]).wait()
    for load in loads:
        load.wait()
    tok = lax.broadcasted_iota(jnp.int32, (A_ROWS, HD), 0) & (ALEN - 1)
    g[0:A_ROWS] = jnp.where(tok < alen, g[0:A_ROWS], jnp.zeros((), BF16))
    tok = me * PIECE + (lax.broadcasted_iota(jnp.int32, (P_ROWS, HD), 0) & (PIECE - 1))
    g[A_ROWS:ROWS] = jnp.where(tok < plen, g[A_ROWS:ROWS], jnp.zeros((), BF16))

    def rows_of(s):
        return pl.multiple_of(s * 256, 256) if not isinstance(s, int) else s * 256

    def limits(j):
        lane = lax.broadcasted_iota(jnp.int32, (1, LANES), 1)
        if j * LANES < A_ROWS:
            return jnp.zeros((1, LANES), jnp.int32) + (plen - 1), lane & (ALEN - 1)
        pos = me * PIECE + (lane & (PIECE - 1))
        return jnp.minimum(pos, plen - 1), jnp.full((1, LANES), -1, jnp.int32)

    def score_group(s, bases, own=False):
        n = PIECE * len(bases) + (ALEN if own else 0)
        rows = pl.ds(rows_of(s), n)
        slots = pl.ds(4 * s, n // PIECE)
        keys = kv[slots, 0].reshape(n, HD)
        values = kv[slots, 1].reshape(n, HD)
        for j in range(CHUNKS):
            lanes = slice(j * LANES, (j + 1) * LANES)
            lim, lim_own = limits(j)
            raw = lax.dot_general(keys, q[lanes, :], NT, preferred_element_type=F32)
            parts = []
            for b, base in enumerate(bases):
                pos = base + lax.broadcasted_iota(jnp.int32, (PIECE, LANES), 0)
                parts.append(jnp.where(pos <= lim, raw[b * PIECE:(b + 1) * PIECE], NEG))
            if own:
                pos = lax.broadcasted_iota(jnp.int32, (ALEN, LANES), 0)
                parts.append(jnp.where(pos <= lim_own, raw[n - ALEN:n], NEG))
            raw = jnp.concatenate(parts, 0).reshape(n // 8, 8, LANES)
            high = jnp.max(raw, axis=0)
            if own:
                new = high
            else:
                old = mrun[:, lanes]
                new = jnp.maximum(old, high)
            ex = jnp.exp2((raw - new[None]) * COEF)
            part = jnp.sum(ex, axis=0)
            if own:
                tot[:, lanes] = part
            else:
                tot[:, lanes] = tot[:, lanes] * jnp.exp2((old - new) * COEF) + part
            mrun[:, lanes] = new
            mgrp[s, :, lanes] = new
            e[rows, lanes] = ex.reshape(n, LANES)
            dp[rows, lanes] = lax.dot_general(values, g[lanes, :], NT, preferred_element_type=F32)

    def bases(f, k):
        half = par if k == 0 else 1 - par
        return [(half * nz + along(-(near_step(f, n) + far_step(f)))) * PIECE for n in range(4)]

    def loop(first, stop, *steps):
        def body(i, carry):
            f = first + i if stop >= first else first - 1 - i
            for step in steps:
                step(f)
            return carry
        lax.fori_loop(0, abs(stop - first), body, 0)

    def loop(first, stop, *steps):
        def body(i, carry):
            f = first + i if stop >= first else first - 1 - i
            for step in steps:
                step(f)
            return carry
        lax.fori_loop(0, abs(stop - first), body, 0)

    def score(f, k):
        score_group(2 * f + k, bases(f, k))

    score_group(last, [], True)
    for f in range(1, fars):
        to_far(f).wait_recv()
        to_cross(f, 0).start()
        for n in range(1, 4):
            to_near(f, 0, n).start()
    for f in range(early):
        spread_cross(f)
        near_arrived(f, 0)
        score(f, 0)
    for f in range(early, fars):
        near_to_cross(f)
    loop(early, fars, lambda f: score(f, 0))
    loop(0, early, lambda f: near_arrived(f, 1), lambda f: score(f, 1))
    loop(early, fars, lambda f: cross_arrived(f), lambda f: score(f, 1))

    m8 = mrun[...]
    top = jnp.max(m8, axis=0, keepdims=True)
    total = jnp.sum(tot[...] * jnp.exp2((m8 - top) * COEF), axis=0, keepdims=True)
    inv = 1.0 / total
    for s in range(last + 1):
        rgrp[s] = jnp.exp2((mgrp[s] - top) * COEF) * inv
    delta[...] = jnp.zeros_like(delta)

    def value_terms(s, n=256):
        rows = pl.ds(rows_of(s), n)
        for j in range(CHUNKS):
            lanes = slice(j * LANES, (j + 1) * LANES)
            p = e[rows, lanes].reshape(n // 8, 8, LANES) * rgrp[s, :, lanes][None]
            pb = p.reshape(n, LANES).astype(BF16)
            pbuf[0:n, lanes] = pb
            prod = pb.astype(F32) * dp[rows, lanes]
            delta[:, lanes] += jnp.sum(prod.reshape(n // 8, 8, LANES), axis=0)
        terms[1, rows, :] = jnp.dot(pbuf[0:n], g[...], preferred_element_type=F32)

    def key_terms(s, n=256):
        rows = pl.ds(rows_of(s), n)
        for j in range(CHUNKS):
            lanes = slice(j * LANES, (j + 1) * LANES)
            p = e[rows, lanes].reshape(n // 8, 8, LANES) * (rgrp[s, :, lanes] * SCALE)[None]
            diff = dp[rows, lanes].reshape(n // 8, 8, LANES) - delta[:, lanes][None]
            ds[rows, lanes] = (p * diff).reshape(n, LANES).astype(BF16)
        terms[0, rows, :] = jnp.dot(ds[rows, :], q[...], preferred_element_type=F32)

    def query_terms(j):
        lanes = slice(j * LANES, (j + 1) * LANES)
        rows = jnp.dot(kt[...], ds[:, lanes], preferred_element_type=F32)
        dq[lanes, :] = rows.T.astype(BF16)

    def sum_cross(c, f):
        rows = pl.ds(0, 256 if f >= early else PIECE)
        return remote(x_out.at[c, f, rows], x_in.at[c, f, rows], sx_send.at[c, f], sx_recv.at[c, f], cross)

    def sum_near(c, f, k, n):
        return remote(near_out.at[c, f, k, n - 1], near_in.at[c, f, k, n - 1],
                      sn_send.at[c, f, k, n - 1], sn_recv.at[c, f, k, n - 1], peer(-near_step(f, n)))

    def sum_far(c, f):
        return remote(far_out.at[c, f - 1], far_in.at[c, f - 1],
                      sf_send.at[c, f - 1], sf_recv.at[c, f - 1], peer(-far_step(f)))

    def send_near(c, f, k):
        if k == 0 and f >= early:
            sum_cross(c, f).wait_recv()
        row = 512 * f + 256 * k
        for n in range(1, 4):
            part = terms[c, row + n * PIECE:row + (n + 1) * PIECE, :]
            if k == 0 and f >= early:
                part = part + x_in[c, f, n * PIECE:(n + 1) * PIECE, :].astype(F32)
            near_out[c, f, k, n - 1] = part.astype(BF16)
            sum_near(c, f, k, n).start()

    def near_sum(c, f, k):
        row = 512 * f + 256 * k
        acc = terms[c, row:row + PIECE, :]
        for n in range(1, 4):
            sum_near(c, f, k, n).wait_recv()
            acc = acc + near_in[c, f, k, n - 1].astype(F32)
        return acc

    def send_cross(c, f):
        if f >= early:
            x_out[c, f] = terms[c, 512 * f + 256:512 * f + 512, :].astype(BF16)
        else:
            x_out[c, f, 0:PIECE] = near_sum(c, f, 1).astype(BF16)
        sum_cross(c, f).start()

    def held(c, f):
        acc = near_sum(c, f, 0)
        if f < early:
            sum_cross(c, f).wait_recv()
        return acc + x_in[c, f, 0:PIECE, :].astype(F32)

    def send_far(c, f):
        far_out[c, f - 1] = held(c, f).astype(BF16)
        sum_far(c, f).start()

    def finish(c):
        acc = held(c, 0)
        for f in range(1, fars):
            sum_far(c, f).wait_recv()
            acc = acc + far_in[c, f - 1].astype(F32)
        prm_out[c] = acc.astype(BF16)

    late_groups = list(range(fars - 1, early - 1, -1))
    early_groups = list(range(early - 1, -1, -1))
    far_groups = list(range(fars - 1, 0, -1))

    for f in late_groups:
        value_terms(2 * f + 1)
        send_cross(V, f)
    for f in early_groups:
        value_terms(2 * f + 1)
        send_near(V, f, 1)
    for f in early_groups:
        value_terms(2 * f)
        send_near(V, f, 0)
    loop(fars, early, lambda f: value_terms(2 * f))
    value_terms(last, 128)
    delta[...] = jnp.broadcast_to(jnp.sum(delta[...], axis=0, keepdims=True), delta.shape)
    for f in late_groups:
        key_terms(2 * f + 1)
        send_cross(K, f)
    for f in late_groups:
        send_near(V, f, 0)
    for f in early_groups:
        key_terms(2 * f + 1)
        send_near(K, f, 1)
    for f in early_groups:
        send_cross(V, f)
    for f in early_groups:
        key_terms(2 * f)
        send_near(K, f, 0)
    loop(fars, early, lambda f: key_terms(2 * f))
    for f in late_groups:
        send_near(K, f, 0)
    key_terms(last, 128)
    own_out[...] = terms[:, 256 * last:256 * last + ALEN, :].astype(BF16)
    own_store = pltpu.make_async_copy(own_out, dkv_a, st_sem.at[0])
    own_store.start()
    for f in far_groups:
        send_far(V, f)
    for f in early_groups:
        send_cross(K, f)
    for s in range(n_keys // 128):
        kt[:, s * 128:(s + 1) * 128] = kv[2 * s:2 * s + 2, 0].reshape(128, HD).T
    for j in range(CHUNKS // 2):
        query_terms(j)
    late_far = far_groups[:1]
    for f in late_far:
        send_far(K, f)
    for j in range(CHUNKS // 2, CHUNKS):
        query_terms(j)
    for f in far_groups:
        if f not in late_far:
            send_far(K, f)
    for h in range(HEADS):
        cols = pl.ds(h * HD, HD)
        pltpu.make_async_copy(dq.at[pl.ds(h * ALEN, ALEN)], dq_a.at[:, cols], st_sem.at[1]).start()
        pltpu.make_async_copy(dq.at[pl.ds(A_ROWS + h * PIECE, PIECE)], dq_p.at[:, cols], st_sem.at[1]).start()

    def sent(c):
        for f in range(fars):
            for k in range(1 if f >= early else 2):
                for n in range(1, 4):
                    sum_near(c, f, k, n).wait_send()
            sum_cross(c, f).wait_send()
            if f:
                sum_far(c, f).wait_send()

    finish(V)
    for f in range(fars):
        for n in range(4 if f >= early else 1):
            to_cross(f, n).wait_send()
        for k in range(1 if f >= early else 2):
            for n in range(1, 4):
                to_near(f, k, n).wait_send()
        if f:
            to_far(f).wait_send()
    sent(V)
    own_store.wait()
    pltpu.make_async_copy(dq, dq, st_sem.at[1]).wait()
    finish(K)
    prompt_store = pltpu.make_async_copy(prm_out, dkv_p, st_sem.at[2])
    prompt_store.start()
    sent(K)
    prompt_store.wait()


def deliver(*refs):
    count = len(refs) // 3
    loads, stores = refs[-2:]
    ins, outs, held = refs[:count], refs[count:2 * count], refs[2 * count:3 * count]
    for i in range(count):
        pltpu.make_async_copy(ins[i], held[i], loads.at[i]).start()
    for i in range(count):
        pltpu.make_async_copy(ins[i], held[i], loads.at[i]).wait()
        pltpu.make_async_copy(held[i], outs[i], stores.at[i]).start()
    for i in range(count):
        pltpu.make_async_copy(held[i], outs[i], stores.at[i]).wait()


def per_device(nz, q_ans, kv_ans, q_prompt, kv_prompt, dout_ans, dout_prompt, ans_len, prompt_len):
    fars = nz // 4
    groups = 2 * fars + 1
    n_keys = 512 * fars + 128
    any_spec = pl.BlockSpec(memory_space=pl.ANY)
    smem = pl.BlockSpec(memory_space=pltpu.SMEM)
    dma, vm = pltpu.SemaphoreType.DMA, pltpu.VMEM
    out_shape = tuple(jax.ShapeDtypeStruct(a.shape, BF16) for a in (q_ans, kv_ans, q_prompt, kv_prompt))
    results = pl.pallas_call(
        functools.partial(kernel, nz),
        out_shape=out_shape,
        in_specs=[smem, smem] + [any_spec] * 6,
        out_specs=(any_spec,) * 4,
        scratch_shapes=[
            vm((n_keys // PIECE, 2, PIECE, HD), BF16),
            vm((HD, n_keys), BF16),
            vm((ROWS, HD), BF16),
            vm((ROWS, HD), BF16),
            vm((n_keys, ROWS), F32),
            vm((n_keys, ROWS), F32),
            vm((n_keys, ROWS), BF16),
            vm((256, ROWS), BF16),
            vm((8, ROWS), F32),
            vm((8, ROWS), F32),
            vm((groups, 8, ROWS), F32),
            vm((groups, 8, ROWS), F32),
            vm((8, ROWS), F32),
            vm((2, n_keys, HD), F32),
            vm((ROWS, HD), BF16),
            vm((2, ALEN, HD), BF16),
            vm((2, PIECE, HD), BF16),
            vm((2, fars, 256, HD), BF16), vm((2, fars, 256, HD), BF16),
            vm((2, fars, 2, 3, PIECE, HD), BF16), vm((2, fars, 2, 3, PIECE, HD), BF16),
            vm((2, fars - 1, PIECE, HD), BF16), vm((2, fars - 1, PIECE, HD), BF16),
            dma((5,)), dma((3,)),
            dma((fars,)), dma((fars,)), dma((fars, 2, 4)), dma((fars, 2, 4)),
            dma((fars, 4)), dma((fars, 4)),
            dma((2, fars - 1)), dma((2, fars - 1)), dma((2, fars, 2, 3)), dma((2, fars, 2, 3)),
            dma((2, fars)), dma((2, fars)),
        ],
        compiler_params=pltpu.CompilerParams(
            collective_id=0, has_side_effects=True, vmem_limit_bytes=58 * 1024 * 1024),
    )(ans_len, prompt_len, q_ans, kv_ans, q_prompt, kv_prompt, dout_ans, dout_prompt)
    return pl.pallas_call(
        deliver, out_shape=out_shape, in_specs=[any_spec] * 4, out_specs=(any_spec,) * 4,
        scratch_shapes=[vm(a.shape, BF16) for a in out_shape] + [dma((4,)), dma((4,))],
    )(*results)


def solution(mesh):
    in_specs = (
        P(("group", "ans"), "tp"),
        P(None, ("group", "ans"), "tp"),
        P(("group", "ans"), "tp"),
        P(None, ("group", "ans"), "tp"),
        P(("group", "ans"), "tp"),
        P(("group", "ans"), "tp"),
        P(("group", "ans")),
        P("group"),
    )
    out_specs = (
        P(("group", "ans"), "tp"),
        P(None, ("group", "ans"), "tp"),
        P(("group", "ans"), "tp"),
        P(None, ("group", "ans"), "tp"),
    )
    return jax.shard_map(
        functools.partial(per_device, mesh.shape["ans"] // 2), mesh=mesh,
        in_specs=in_specs, out_specs=out_specs, check_vma=False)
```
